128 devices in a mesh: row: 8 (over y, core), col: 16 (over z, x).
Axes of the slice: x: 4, y: 4, z: 4, core: 2. Of those that a mesh axis runs over, the one named last changes fastest.
Arguments:
- leaf_rhs: float32 [512, 262144], P(None, ('row', 'col')), may hold values from -6 to 6
- top_rhs: float32 [512, 2048], P('col', 'row'), may hold values from -6 to 6
- leaf_inverse: float32 [1024, 256, 256], P(('row', 'col')), as said below
- leaf_blocks: float32 [1024, 4, 256, 256], P(('row', 'col')), may hold values from -0.015625 to 0.015625
- leaf_targets: int32 [1024, 4], P(('row', 'col')), may hold values from 0 to 7, as said below
- leaf_live: int32 [1024], P(('row', 'col')), may hold values from 1 to 4
- top_blocks: float32 [8, 8, 256, 256], P('row'), as said below
Outputs:
- leaf_solution: float32 [512, 262144], P(None, ('row', 'col'))
- top_solution: float32 [512, 2048], P('col', 'row')
The draws below stay inside these ranges and needn't reach their ends.
Inputs may be any that keep to these rules, and one draw needn't show every extreme that they name: `leaf_targets`: the 4 targets of one leaf are distinct. `leaf_inverse`: lower triangular blocks with positive diagonal. `top_blocks`: diagonal entries [t, t] are lower triangular with positive diagonal.
All inputs are finite; a program needn't handle non-finite values.
Results may differ from the reference program's by a relative error of at most 0.0003.
Values sent between devices are 32-bit elements; how exact they have to be, the bound alone decides.
A program may use at most 128 MiB of HBM per device.

```python
import math
import jax
import jax.numpy as jnp
from jax import lax

B = 256
R = 512
LEAF_DEV = 8
NOFF = 4
NTOP = 8
NLEAF = 1024
N_COL = 16


def lower_shape(noise, diag_values):
    rows = jnp.arange(B)[:, None]
    cols = jnp.arange(B)[None, :]
    below = jnp.where(rows > cols, noise * (0.6 / math.sqrt(B)), 0.0)
    return jnp.where(rows == cols, diag_values, below)


def draw_leaf_inverse(key, part):
    key = jax.random.fold_in(key, 11)
    first_key, second_key = jax.random.split(key)
    noise = jax.random.normal(first_key, (NLEAF, B, B), jnp.float32)
    diag_values = jnp.exp(jax.random.uniform(second_key, (NLEAF, B, 1), jnp.float32, math.log(0.5), math.log(2.0)))
    return lower_shape(noise, diag_values)


def draw_top_blocks(key, part):
    key = jax.random.fold_in(key, 23)
    first_key, second_key, third_key = jax.random.split(key, 3)
    noise = jax.random.normal(first_key, (NTOP, NTOP, B, B), jnp.float32)
    outside = jax.random.normal(third_key, (NTOP, NTOP, B, B), jnp.float32)
    diag_values = jnp.exp(jax.random.uniform(second_key, (NTOP, NTOP, B, 1), jnp.float32, math.log(0.5), math.log(2.0)))
    diagonal_blocks = lower_shape(noise, diag_values)
    column_index = jnp.arange(NTOP)[:, None, None, None]
    row_index = jnp.arange(NTOP)[None, :, None, None]
    scaled = outside * (1.0 / math.sqrt(B * NTOP))
    return jnp.where(column_index == row_index, diagonal_blocks, scaled)


def draw_leaf_targets(key, part):
    key = jax.random.fold_in(key, 37)
    leaf_keys = jax.random.split(key, NLEAF)

    def one_leaf(leaf_key):
        return jax.random.permutation(leaf_key, NTOP)[:NOFF]
    picked = jax.vmap(one_leaf)(leaf_keys).astype(jnp.int32)
    ascending = jnp.arange(NOFF, dtype=jnp.int32)
    picked = picked.at[0].set(ascending)
    picked = picked.at[1].set(NTOP - 1 - ascending)
    return picked


def draw_leaf_live(key, part):
    key = jax.random.fold_in(key, 53)
    counts = jax.random.randint(key, (NLEAF,), 1, NOFF + 1, dtype=jnp.int32)
    counts = counts.at[0].set(NOFF)
    counts = counts.at[NLEAF - 1].set(1)
    return counts


def block_scale(own_key, dims, pieces, smallest, top_value):
    factor_of = 1.0
    for dim, shards_of in pieces:
        draws = jax.random.uniform(jax.random.fold_in(jax.random.fold_in(own_key, 6), dim), (shards_of,), jnp.float32, smallest / len(pieces), top_value / len(pieces))
        factor_of = factor_of * jnp.repeat(jnp.exp(draws), dims[dim] // shards_of).reshape((-1,) + (1,) * (len(dims) - 1 - dim))
    return factor_of


def centred(stream_key, shape, width, bound, cuts=(), held_as=jnp.bfloat16):
    values = jax.random.normal(stream_key, shape, jnp.float32) * width
    if len(cuts) > 0:
        values = block_scale(stream_key, shape, cuts, -0.22, 0.18) * values
    return jnp.clip(values, min=-bound, max=bound).astype(held_as)


def setup_inputs(seed: int = 0) -> dict:
    arg_keys = jax.random.split(jax.random.key(seed), 8)
    return {
        "leaf_rhs": centred(arg_keys[0], (R, NLEAF * B), 1.0, 6.0, ((1, 128),), jnp.float32),
        "top_rhs": centred(arg_keys[1], (R, NTOP * B), 1.0, 6.0, ((0, 16), (1, 8)), jnp.float32),
        "leaf_inverse": draw_leaf_inverse(jax.random.fold_in(arg_keys[7], 71), 0),
        "leaf_blocks": centred(arg_keys[3], (NLEAF, NOFF, B, B), (B * LEAF_DEV * N_COL * NOFF) ** -0.5, 0.015625, ((0, 128),), jnp.float32),
        "leaf_targets": draw_leaf_targets(jax.random.fold_in(arg_keys[7], 71), 0),
        "leaf_live": draw_leaf_live(jax.random.fold_in(arg_keys[7], 71), 0),
        "top_blocks": draw_top_blocks(jax.random.fold_in(arg_keys[7], 71), 0),
    }


exact_mode = lax.Precision.HIGHEST


def reference(leaf_rhs, top_rhs, leaf_inverse, leaf_blocks, leaf_targets, leaf_live, top_blocks):
    leaves = leaf_inverse.shape[0]
    supernode = leaf_inverse.shape[1]
    columns = leaf_rhs.shape[0]
    levels = top_blocks.shape[0]
    slot_range = jnp.arange(leaf_blocks.shape[1], dtype=jnp.int32)
    top_range = jnp.arange(levels, dtype=jnp.int32)
    rhs_leaf = leaf_rhs.reshape(columns, leaves, supernode).transpose(1, 0, 2)

    def selector(targets, live):
        picked = (targets[:, None] == top_range[None, :]).astype(jnp.float32)
        return picked * (slot_range < live).astype(jnp.float32)[:, None]

    def forward_leaf(upward, items):
        rhs_one, inverse, blocks, targets, live = items
        solved = jnp.dot(rhs_one, inverse.T, precision=exact_mode)
        products = jnp.einsum("rb,jcb->jrc", solved, blocks, precision=exact_mode)
        upward = upward + jnp.einsum("jn,jrc->nrc", selector(targets, live), products, precision=exact_mode)
        return upward, solved

    start_sum = jnp.zeros((levels, columns, supernode), jnp.float32)
    upward, solved_leaf = lax.scan(forward_leaf, start_sum, (rhs_leaf, leaf_inverse, leaf_blocks, leaf_targets, leaf_live))
    remaining = top_rhs.reshape(columns, levels, supernode).transpose(1, 0, 2) - upward
    running = [remaining[place] for place in range(levels)]
    solved_top = []
    for step_index in range(levels):
        current = jnp.dot(running[step_index], top_blocks[step_index, step_index].T, precision=exact_mode)
        solved_top.append(current)
        for later in range(step_index + 1, levels):
            running[later] = running[later] - jnp.dot(current, top_blocks[step_index, later].T, precision=exact_mode)
    back_sums = list(solved_top)
    top_parts = [None] * levels
    for step_index in reversed(range(levels)):
        current = jnp.dot(back_sums[step_index], top_blocks[step_index, step_index], precision=exact_mode)
        top_parts[step_index] = current
        for earlier in range(step_index):
            back_sums[earlier] = back_sums[earlier] - jnp.dot(current, top_blocks[earlier, step_index], precision=exact_mode)
    stacked = jnp.stack(top_parts)

    def backward_leaf(items):
        solved, inverse, blocks, targets, live = items
        chosen = jnp.einsum("jn,nrb->jrb", selector(targets, live), stacked, precision=exact_mode)
        correction = jnp.einsum("jrb,jbc->rc", chosen, blocks, precision=exact_mode)
        return jnp.dot(solved - correction, inverse, precision=exact_mode)

    leaf_parts = lax.map(backward_leaf, (solved_leaf, leaf_inverse, leaf_blocks, leaf_targets, leaf_live))
    leaf_solution = leaf_parts.transpose(1, 0, 2).reshape(columns, leaves * supernode)
    top_solution = stacked.transpose(1, 0, 2).reshape(columns, levels * supernode)
    return (leaf_solution, top_solution)
```

```python
import functools

import jax
import jax.numpy as jnp
from jax import lax
from jax.experimental import pallas as pl
from jax.experimental.pallas import tpu as pltpu
from jax.sharding import PartitionSpec as P

MESH = pl.DeviceIdType.MESH
exact = lax.Precision.HIGHEST
three_pass = lax.Precision.HIGH

PAIRS = 4
PLANE = 16
HALF = 16


def dot_t(a, b):
    return lax.dot_general(a, b, (((1,), (1,)), ((), ())), precision=exact, preferred_element_type=jnp.float32)


def dot_n(a, b):
    return lax.dot_general(a, b, (((1,), (0,)), ((), ())), precision=exact, preferred_element_type=jnp.float32)


def top_kernel(
    u_ref, rhs_ref, blocks_ref, x_ref, own_ref,
    pair_in, chip_sum, plane_in, plane_sum, y_in, update_out, update_in, blocks, rhs, solved,
    local_sem, blocks_s, blocks_r, rhs_s, rhs_r, pair_s, pair_r, plane_s, plane_r, y_s, y_r, update_s, update_r,
    spread_s, spread_r, out_s, out_r, swap_s, swap_r,
):
    row = lax.axis_index("row")
    col = lax.axis_index("col")
    core = lax.rem(row, 2)
    y = lax.div(row, 2)
    other = 1 - core
    mate = {"row": 2 * y + other}

    def on_y(chip):
        return {"row": 2 * chip + core}

    def on_plane(step):
        return {"col": lax.rem(col + step, PLANE)}

    def remote(src, dst, send, recv, device):
        return pltpu.make_async_remote_copy(
            src_ref=src, dst_ref=dst, send_sem=send, recv_sem=recv, device_id=device, device_id_type=MESH
        )

    barrier = pltpu.get_barrier_semaphore()
    pl.semaphore_signal(barrier, inc=1, device_id=mate, device_id_type=MESH)
    for step in range(1, PAIRS):
        pl.semaphore_signal(barrier, inc=1, device_id=on_y(lax.rem(y + step, PAIRS)), device_id_type=MESH)
    for step in range(1, PLANE):
        pl.semaphore_signal(barrier, inc=1, device_id=on_plane(step), device_id_type=MESH)
    pl.semaphore_wait(barrier, 1 + PAIRS - 1 + PLANE - 1)

    pair_copies = [
        remote(u_ref.at[p, :, :, other], pair_in.at[p], pair_s.at[p], pair_r.at[p], mate) for p in range(PAIRS)
    ]
    for copy in pair_copies:
        copy.start()
    rhs_copy = remote(rhs_ref.at[other], rhs.at[core], rhs_s, rhs_r, mate)
    rhs_copy.start()
    blocks_copy = remote(blocks_ref, blocks.at[core], blocks_s, blocks_r, mate)
    blocks_copy.start()
    local_copy = pltpu.make_async_copy(blocks_ref, blocks.at[core], local_sem)
    local_copy.start()
    rhs[core] = rhs_ref[core]

    plane_copies = []
    for p in range(PAIRS):
        pair_copies[p].wait_recv()
        for level in range(2):
            chip_sum[p, :, level] = u_ref[p, level, :, core] + pair_in[p, level]
        for step in range(1, PLANE):
            copy = remote(
                chip_sum.at[p, lax.rem(col + step, PLANE)], plane_in.at[p, step - 1],
                plane_s.at[p, step - 1], plane_r.at[p, step - 1], on_plane(step),
            )
            copy.start()
            plane_copies.append(copy)
    y_copies = []
    for p in range(PAIRS):
        for step in range(1, PLANE):
            plane_copies[p * (PLANE - 1) + step - 1].wait_recv()
        plane_sum[p] = chip_sum[p, col] + jnp.sum(plane_in[p], axis=0)
        copy = remote(plane_sum.at[p], y_in.at[y], y_s.at[p], y_r.at[y], on_y(p))
        y_copies.append(copy)

        @pl.when(y != p)
        def _():
            copy.start()

    rhs_copy.wait_recv()
    remote(blocks_ref, blocks.at[other], blocks_s, blocks_r, mate).wait_recv()
    local_copy.wait()
    running = [rhs[level] - plane_sum[y, level] for level in range(2)]
    y_in[y] = jnp.zeros((2, HALF, 256), jnp.float32)
    for chip in range(PAIRS):

        @pl.when(y != chip)
        def _():
            remote(plane_sum.at[chip], y_in.at[chip], y_s.at[chip], y_r.at[chip], on_y(chip)).wait_recv()

    solved[0] = running[0] - (y_in[0, 0] + y_in[1, 0] + y_in[2, 0] + y_in[3, 0])
    solved[1] = running[1] - (y_in[0, 1] + y_in[1, 1] + y_in[2, 1] + y_in[3, 1])

    def update_copy(source, target):
        return remote(update_out.at[target], update_in.at[source], update_s.at[target], update_r.at[source], on_y(target))

    for chip in range(PAIRS - 1):

        @pl.when(y > chip)
        def _():
            update_copy(chip, y).wait_recv()
            solved[...] = solved[...] - update_in[chip]

    first = dot_t(solved[0], blocks[0, 2 * y])
    second = dot_t(solved[1] - dot_t(first, blocks[0, 2 * y + 1]), blocks[1, 2 * y + 1])
    solved[0] = first
    solved[1] = second
    for chip in range(1, PAIRS):

        @pl.when(y < chip)
        def _():
            for level in range(2):
                update_out[chip, level] = dot_t(solved[0], blocks[0, 2 * chip + level]) + dot_t(
                    solved[1], blocks[1, 2 * chip + level]
                )
            update_copy(y, chip).start()

    def spread(p, step):
        chunk = x_ref.at[p, :, col, core]
        return remote(chunk, chunk, spread_s.at[step - 1], spread_r.at[p], on_y(lax.rem(y + step, PAIRS)))

    def solve_own():
        second = dot_n(solved[1], blocks[1, 2 * y + 1])
        first = dot_n(solved[0] - dot_n(second, blocks[0, 2 * y + 1]), blocks[0, 2 * y])
        x_ref[y, 0, col, core] = first
        x_ref[y, 1, col, core] = second
        for step in range(1, PAIRS):
            spread(y, step).start()

    def out_copy(p, step):
        chunk = x_ref.at[p, :, col, core]
        return remote(chunk, chunk, out_s.at[p, step - 1], out_r.at[p, step - 1], on_plane(step))

    def out_wait(p, step):
        chunk = x_ref.at[p, :, lax.rem(col + PLANE - step, PLANE), core]
        remote(chunk, chunk, out_s.at[p, step - 1], out_r.at[p, step - 1], on_plane(step)).wait_recv()

    def swap_copy(p, half):
        part = x_ref.at[p, :, :, half]
        return remote(part, part, swap_s.at[p], swap_r.at[p], mate)

    def finish(p):
        for step in range(1, PLANE):
            out_wait(p, step)
        swap_copy(p, core).start()

    @pl.when(y == PAIRS - 1)
    def _():
        solve_own()

    for p in reversed(range(PAIRS)):

        @pl.when(y != p)
        def _():
            spread(p, 1).wait_recv()

        @pl.when(y < p)
        def _():
            for level in range(2):
                piece = x_ref[p, level, col, core]
                solved[0] = solved[0] - dot_n(piece, blocks[0, 2 * p + level])
                solved[1] = solved[1] - dot_n(piece, blocks[1, 2 * p + level])

        if p > 0:

            @pl.when(y == p - 1)
            def _():
                solve_own()

        for step in range(1, PLANE):
            out_copy(p, step).start()
        if p < PAIRS - 1:
            finish(p + 1)
    finish(0)
    for p in range(PAIRS):
        swap_copy(p, other).wait_recv()
    own_ref[...] = x_ref[y, core, col]

    rhs_copy.wait_send()
    blocks_copy.wait_send()
    for copy in pair_copies:
        copy.wait_send()
    for copy in plane_copies:
        copy.wait_send()
    for p in range(PAIRS):

        @pl.when(y != p)
        def _():
            y_copies[p].wait_send()

    for chip in range(1, PAIRS):

        @pl.when(y < chip)
        def _():
            update_copy(y, chip).wait_send()

    for step in range(1, PAIRS):
        spread(y, step).wait_send()
    for p in range(PAIRS):
        for step in range(1, PLANE):
            out_copy(p, step).wait_send()
        swap_copy(p, core).wait_send()


def top_solve(upward, rhs, blocks):
    f32 = jnp.float32
    dma = pltpu.SemaphoreType.DMA
    vmem = pl.BlockSpec(memory_space=pltpu.VMEM)
    return pl.pallas_call(
        top_kernel,
        out_shape=(
            jax.ShapeDtypeStruct((PAIRS, 2, PLANE, 2, HALF, 256), f32),
            jax.ShapeDtypeStruct((2, HALF, 256), f32),
        ),
        in_specs=[vmem, vmem, pl.BlockSpec(memory_space=pl.ANY)],
        out_specs=(vmem, vmem),
        scratch_shapes=[
            pltpu.VMEM((PAIRS, 2, PLANE, HALF, 256), f32),
            pltpu.VMEM((PAIRS, PLANE, 2, HALF, 256), f32),
            pltpu.VMEM((PAIRS, PLANE - 1, 2, HALF, 256), f32),
            pltpu.VMEM((PAIRS, 2, HALF, 256), f32),
            pltpu.VMEM((PAIRS, 2, HALF, 256), f32),
            pltpu.VMEM((PAIRS, 2, HALF, 256), f32),
            pltpu.VMEM((PAIRS, 2, HALF, 256), f32),
            pltpu.VMEM((2, 8, 256, 256), f32),
            pltpu.VMEM((2, HALF, 256), f32),
            pltpu.VMEM((2, HALF, 256), f32),
            dma,
            dma, dma, dma, dma,
            dma((PAIRS,)), dma((PAIRS,)),
            dma((PAIRS, PLANE - 1)), dma((PAIRS, PLANE - 1)),
            dma((PAIRS,)), dma((PAIRS,)),
            dma((PAIRS,)), dma((PAIRS,)),
            dma((PAIRS,)), dma((PAIRS,)),
            dma((PAIRS, PLANE - 1)), dma((PAIRS, PLANE - 1)),
            dma((PAIRS,)), dma((PAIRS,)),
        ],
        compiler_params=pltpu.CompilerParams(
            collective_id=0, has_side_effects=True, vmem_limit_bytes=40 * 1024 * 1024
        ),
        cost_estimate=pl.CostEstimate(flops=10**9, bytes_accessed=10**7, transcendentals=0),
    )(upward, rhs, blocks)


def on_device(leaf_rhs, top_rhs, leaf_inverse, leaf_blocks, leaf_targets, leaf_live, top_blocks):
    columns = leaf_rhs.shape[0]
    leaves = leaf_inverse.shape[0]
    supernode = leaf_inverse.shape[1]
    slots = leaf_blocks.shape[1]
    levels = lax.axis_size("row")
    rhs_blocks = leaf_rhs.reshape(columns, leaves, supernode)
    solved = jnp.einsum("rkb,kcb->krc", rhs_blocks, leaf_inverse, precision=three_pass)
    used = (jnp.arange(slots, dtype=jnp.int32)[None, :] < leaf_live[:, None]).astype(jnp.float32)
    picked = (
        leaf_targets[:, :, None] == jnp.arange(levels, dtype=jnp.int32)[None, None, :]
    ).astype(jnp.float32)
    weights = picked * used[:, :, None]
    partial_terms = jnp.einsum("krb,kjcb->kjrc", solved, leaf_blocks, precision=three_pass)
    upward = jnp.einsum("kjn,kjrc->nrc", weights, partial_terms, precision=three_pass)
    whole, own = top_solve(
        upward.reshape(PAIRS, 2, PLANE, 2, HALF, supernode), top_rhs.reshape(2, HALF, supernode), top_blocks[0]
    )
    top_whole = whole.reshape(levels, columns, supernode)
    chosen = jnp.einsum("kjn,nrb->kjrb", weights, top_whole, precision=three_pass)
    correction = jnp.einsum("kjrb,kjbc->krc", chosen, leaf_blocks, precision=three_pass)
    leaf_parts = jnp.einsum("krb,kbc->krc", solved - correction, leaf_inverse, precision=three_pass)
    leaf_solution = leaf_parts.transpose(1, 0, 2).reshape(columns, leaves * supernode)
    return (leaf_solution, own.reshape(2 * HALF, supernode))


def solution(mesh):
    in_specs = (
        P(None, ("row", "col")),
        P("col", "row"),
        P(("row", "col"), None, None),
        P(("row", "col"), None, None, None),
        P(("row", "col"), None),
        P(("row", "col")),
        P("row", None, None, None),
    )
    out_specs = (P(None, ("row", "col")), P("col", "row"))
    return jax.shard_map(
        on_device, mesh=mesh, in_specs=in_specs, out_specs=out_specs, check_vma=False
    )
```

```python
import functools

import jax
import jax.numpy as jnp
from jax import lax
from jax.experimental import pallas as pl
from jax.experimental.pallas import tpu as pltpu
from jax.sharding import PartitionSpec as P

MESH = pl.DeviceIdType.MESH
exact = lax.Precision.HIGHEST
three_pass = lax.Precision.HIGH

PAIRS = 4
HALF = 16


def dot_t(a, b):
    return lax.dot_general(a, b, (((1,), (1,)), ((), ())), precision=exact, preferred_element_type=jnp.float32)


def dot_n(a, b):
    return lax.dot_general(a, b, (((1,), (0,)), ((), ())), precision=exact, preferred_element_type=jnp.float32)


def top_kernel(
    u_ref, rhs_ref, blocks_ref, x_ref, own_ref,
    pair_in, chip_sum, first_in, middle, second_in, plane_sum, y_in, update_out, update_in, blocks, rhs, solved,
    local_sem, blocks_s, blocks_r, rhs_s, rhs_r, pair_s, pair_r, first_s, first_r, second_s, second_r, y_s, y_r, update_s, update_r,
    spread_s, spread_r, chunk_s, chunk_r, line_s, line_r, swap_s, swap_r,
):
    row = lax.axis_index("row")
    col = lax.axis_index("col")
    core = lax.rem(row, 2)
    y = lax.div(row, 2)
    other = 1 - core
    z = lax.div(col, 4)
    x = lax.rem(col, 4)
    mate = {"row": 2 * y + other}

    def on_y(chip):
        return {"row": 2 * chip + core}

    def on_x(step):
        return {"col": 4 * z + lax.rem(x + step, 4)}

    def on_z(step):
        return {"col": 4 * lax.rem(z + step, 4) + x}

    def remote(src, dst, send, recv, device):
        return pltpu.make_async_remote_copy(
            src_ref=src, dst_ref=dst, send_sem=send, recv_sem=recv, device_id=device, device_id_type=MESH
        )

    barrier = pltpu.get_barrier_semaphore()
    pl.semaphore_signal(barrier, inc=1, device_id=mate, device_id_type=MESH)
    for step in range(1, PAIRS):
        pl.semaphore_signal(barrier, inc=1, device_id=on_y(lax.rem(y + step, PAIRS)), device_id_type=MESH)
    for step in range(1, 4):
        pl.semaphore_signal(barrier, inc=1, device_id=on_x(step), device_id_type=MESH)
        pl.semaphore_signal(barrier, inc=1, device_id=on_z(step), device_id_type=MESH)
    pl.semaphore_wait(barrier, 10)

    pair_copies = [
        remote(u_ref.at[p, :, :, :, other], pair_in.at[p], pair_s.at[p], pair_r.at[p], mate) for p in range(PAIRS)
    ]
    for copy in pair_copies:
        copy.start()
    rhs_copy = remote(rhs_ref.at[other], rhs.at[core], rhs_s, rhs_r, mate)
    rhs_copy.start()
    blocks_copy = remote(blocks_ref, blocks.at[core], blocks_s, blocks_r, mate)
    blocks_copy.start()
    local_copy = pltpu.make_async_copy(blocks_ref, blocks.at[core], local_sem)
    local_copy.start()
    rhs[core] = rhs_ref[core]

    def first_copy(p, level, step):
        if level == 0:
            src, device = chip_sum.at[p, 0, :, lax.rem(x + step, 4)], on_x(step)
        else:
            src, device = chip_sum.at[p, 1, lax.rem(z + step, 4)], on_z(step)
        return remote(
            src, first_in.at[p, level, step - 1], first_s.at[p, level, step - 1], first_r.at[p, level, step - 1], device
        )

    def second_copy(p, level, step):
        if level == 0:
            src, device = middle.at[p, 0, lax.rem(z + step, 4)], on_z(step)
        else:
            src, device = middle.at[p, 1, lax.rem(x + step, 4)], on_x(step)
        return remote(
            src, second_in.at[p, level, step - 1],
            second_s.at[p, level, step - 1], second_r.at[p, level, step - 1], device,
        )

    def y_copy(p, source):
        return remote(plane_sum.at[p], y_in.at[source], y_s.at[p], y_r.at[source], on_y(p))

    both = [(level, step) for step in (2, 1, 3) for level in range(2)]
    for p in range(PAIRS):
        pair_copies[p].wait_recv()
        chip_sum[p] = u_ref[p, :, :, :, core] + pair_in[p]
        for level, step in both:
            first_copy(p, level, step).start()
    for p in range(PAIRS):
        for level, step in both:
            first_copy(p, level, step).wait_recv()
        middle[p, 0] = chip_sum[p, 0, :, x] + first_in[p, 0, 0] + first_in[p, 0, 1] + first_in[p, 0, 2]
        middle[p, 1] = chip_sum[p, 1, z] + first_in[p, 1, 0] + first_in[p, 1, 1] + first_in[p, 1, 2]
        for level, step in both:
            second_copy(p, level, step).start()
    for p in range(PAIRS):
        for level, step in both:
            second_copy(p, level, step).wait_recv()
        plane_sum[p, 0] = middle[p, 0, z] + second_in[p, 0, 0] + second_in[p, 0, 1] + second_in[p, 0, 2]
        plane_sum[p, 1] = middle[p, 1, x] + second_in[p, 1, 0] + second_in[p, 1, 1] + second_in[p, 1, 2]

        @pl.when(y != p)
        def _():
            y_copy(p, y).start()

    rhs_copy.wait_recv()
    remote(blocks_ref, blocks.at[other], blocks_s, blocks_r, mate).wait_recv()
    local_copy.wait()
    running = [rhs[level] - plane_sum[y, level] for level in range(2)]
    y_in[y] = jnp.zeros((2, HALF, 256), jnp.float32)
    for chip in range(PAIRS):

        @pl.when(y != chip)
        def _():
            y_copy(chip, chip).wait_recv()

    solved[0] = running[0] - (y_in[0, 0] + y_in[1, 0] + y_in[2, 0] + y_in[3, 0])
    solved[1] = running[1] - (y_in[0, 1] + y_in[1, 1] + y_in[2, 1] + y_in[3, 1])

    def update_copy(source, target):
        return remote(update_out.at[target], update_in.at[source], update_s.at[target], update_r.at[source], on_y(target))

    for chip in range(PAIRS - 1):

        @pl.when(y > chip)
        def _():
            update_copy(chip, y).wait_recv()
            solved[...] = solved[...] - update_in[chip]

    first = dot_t(solved[0], blocks[0, 2 * y])
    second = dot_t(solved[1] - dot_t(first, blocks[0, 2 * y + 1]), blocks[1, 2 * y + 1])
    solved[0] = first
    solved[1] = second
    for chip in range(1, PAIRS):

        @pl.when(y < chip)
        def _():
            for level in range(2):
                update_out[chip, level] = dot_t(solved[0], blocks[0, 2 * chip + level]) + dot_t(
                    solved[1], blocks[1, 2 * chip + level]
                )
            update_copy(y, chip).start()

    def spread(p, step):
        chunk = x_ref.at[p, :, z, x, core]
        return remote(chunk, chunk, spread_s.at[step - 1], spread_r.at[p], on_y(lax.rem(y + step, PAIRS)))

    def solve_own():
        second = dot_n(solved[1], blocks[1, 2 * y + 1])
        first = dot_n(solved[0] - dot_n(second, blocks[0, 2 * y + 1]), blocks[0, 2 * y])
        x_ref[y, 0, z, x, core] = first
        x_ref[y, 1, z, x, core] = second
        for step in range(1, PAIRS):
            spread(y, step).start()

    def chunk_copy(p, level, step):
        chunk = x_ref.at[p, level, z, x, core]
        device = on_z(step) if level == 0 else on_x(step)
        return remote(chunk, chunk, chunk_s.at[p, level, step - 1], chunk_r.at[p, level, step - 1], device)

    def line_copy(p, level, step):
        if level == 0:
            line, device = x_ref.at[p, 0, :, x, core], on_x(step)
        else:
            line, device = x_ref.at[p, 1, z, :, core], on_z(step)
        return remote(line, line, line_s.at[p, level, step - 1], line_r.at[p, level, step - 1], device)

    def send_lines(p):
        for level, step in both:
            chunk_copy(p, level, step).wait_recv()
        for level, step in both:
            line_copy(p, level, step).start()

    def swap_copy(p, half):
        part = x_ref.at[p, :, :, :, half]
        return remote(part, part, swap_s.at[p], swap_r.at[p], mate)

    def finish(p):
        for level, step in both:
            line_copy(p, level, step).wait_recv()
        swap_copy(p, core).start()

    @pl.when(y == PAIRS - 1)
    def _():
        solve_own()

    for p in reversed(range(PAIRS)):

        @pl.when(y != p)
        def _():
            spread(p, 1).wait_recv()

        @pl.when(y < p)
        def _():
            for level in range(2):
                piece = x_ref[p, level, z, x, core]
                solved[0] = solved[0] - dot_n(piece, blocks[0, 2 * p + level])
                solved[1] = solved[1] - dot_n(piece, blocks[1, 2 * p + level])

        if p > 0:

            @pl.when(y == p - 1)
            def _():
                solve_own()

        for level, step in both:
            chunk_copy(p, level, step).start()
        if p + 1 < PAIRS:
            send_lines(p + 1)
        if p + 2 < PAIRS:
            finish(p + 2)
    send_lines(0)
    finish(1)
    finish(0)
    for p in range(PAIRS):
        swap_copy(p, other).wait_recv()
    own_ref[...] = x_ref[y, core, z, x]

    rhs_copy.wait_send()
    blocks_copy.wait_send()
    for copy in pair_copies:
        copy.wait_send()
    for p in range(PAIRS):
        for level, step in both:
            first_copy(p, level, step).wait_send()
            second_copy(p, level, step).wait_send()
            chunk_copy(p, level, step).wait_send()
            line_copy(p, level, step).wait_send()
        swap_copy(p, core).wait_send()

        @pl.when(y != p)
        def _():
            y_copy(p, y).wait_send()

    for chip in range(1, PAIRS):

        @pl.when(y < chip)
        def _():
            update_copy(y, chip).wait_send()

    for step in range(1, PAIRS):
        spread(y, step).wait_send()


def top_solve(upward, rhs, blocks):
    f32 = jnp.float32
    dma = pltpu.SemaphoreType.DMA
    vmem = pl.BlockSpec(memory_space=pltpu.VMEM)
    return pl.pallas_call(
        top_kernel,
        out_shape=(
            jax.ShapeDtypeStruct((PAIRS, 2, 4, 4, 2, HALF, 256), f32),
            jax.ShapeDtypeStruct((2, HALF, 256), f32),
        ),
        in_specs=[vmem, vmem, pl.BlockSpec(memory_space=pl.ANY)],
        out_specs=(vmem, vmem),
        scratch_shapes=[
            pltpu.VMEM((PAIRS, 2, 4, 4, HALF, 256), f32),
            pltpu.VMEM((PAIRS, 2, 4, 4, HALF, 256), f32),
            pltpu.VMEM((PAIRS, 2, 3, 4, HALF, 256), f32),
            pltpu.VMEM((PAIRS, 2, 4, HALF, 256), f32),
            pltpu.VMEM((PAIRS, 2, 3, HALF, 256), f32),
            pltpu.VMEM((PAIRS, 2, HALF, 256), f32),
            pltpu.VMEM((PAIRS, 2, HALF, 256), f32),
            pltpu.VMEM((PAIRS, 2, HALF, 256), f32),
            pltpu.VMEM((PAIRS, 2, HALF, 256), f32),
            pltpu.VMEM((2, 8, 256, 256), f32),
            pltpu.VMEM((2, HALF, 256), f32),
            pltpu.VMEM((2, HALF, 256), f32),
            dma,
            dma, dma, dma, dma,
            dma((PAIRS,)), dma((PAIRS,)),
            dma((PAIRS, 2, 3)), dma((PAIRS, 2, 3)),
            dma((PAIRS, 2, 3)), dma((PAIRS, 2, 3)),
            dma((PAIRS,)), dma((PAIRS,)),
            dma((PAIRS,)), dma((PAIRS,)),
            dma((PAIRS,)), dma((PAIRS,)),
            dma((PAIRS, 2, 3)), dma((PAIRS, 2, 3)),
            dma((PAIRS, 2, 3)), dma((PAIRS, 2, 3)),
            dma((PAIRS,)), dma((PAIRS,)),
        ],
        compiler_params=pltpu.CompilerParams(
            collective_id=0, has_side_effects=True, vmem_limit_bytes=40 * 1024 * 1024
        ),
        cost_estimate=pl.CostEstimate(flops=10**9, bytes_accessed=10**7, transcendentals=0),
    )(upward, rhs, blocks)


def on_device(leaf_rhs, top_rhs, leaf_inverse, leaf_blocks, leaf_targets, leaf_live, top_blocks):
    columns = leaf_rhs.shape[0]
    leaves = leaf_inverse.shape[0]
    supernode = leaf_inverse.shape[1]
    slots = leaf_blocks.shape[1]
    levels = lax.axis_size("row")
    rhs_blocks = leaf_rhs.reshape(columns, leaves, supernode)
    solved = jnp.einsum("rkb,kcb->krc", rhs_blocks, leaf_inverse, precision=three_pass)
    used = (jnp.arange(slots, dtype=jnp.int32)[None, :] < leaf_live[:, None]).astype(jnp.float32)
    picked = (
        leaf_targets[:, :, None] == jnp.arange(levels, dtype=jnp.int32)[None, None, :]
    ).astype(jnp.float32)
    weights = picked * used[:, :, None]
    partial_terms = jnp.einsum("krb,kjcb->kjrc", solved, leaf_blocks, precision=three_pass)
    upward = jnp.einsum("kjn,kjrc->nrc", weights, partial_terms, precision=three_pass)
    whole, own = top_solve(
        upward.reshape(PAIRS, 2, 4, 4, 2, HALF, supernode), top_rhs.reshape(2, HALF, supernode), top_blocks[0]
    )
    top_whole = whole.reshape(levels, columns, supernode)
    chosen = jnp.einsum("kjn,nrb->kjrb", weights, top_whole, precision=three_pass)
    correction = jnp.einsum("kjrb,kjbc->krc", chosen, leaf_blocks, precision=three_pass)
    leaf_parts = jnp.einsum("krb,kbc->krc", solved - correction, leaf_inverse, precision=three_pass)
    leaf_solution = leaf_parts.transpose(1, 0, 2).reshape(columns, leaves * supernode)
    return (leaf_solution, own.reshape(2 * HALF, supernode))


def solution(mesh):
    in_specs = (
        P(None, ("row", "col")),
        P("col", "row"),
        P(("row", "col"), None, None),
        P(("row", "col"), None, None, None),
        P(("row", "col"), None),
        P(("row", "col")),
        P("row", None, None, None),
    )
    out_specs = (P(None, ("row", "col")), P("col", "row"))
    return jax.shard_map(
        on_device, mesh=mesh, in_specs=in_specs, out_specs=out_specs, check_vma=False
    )
```

```python
import jax
import jax.numpy as jnp
from jax import lax
from jax.experimental import pallas as pl
from jax.experimental.pallas import tpu as pltpu
from jax.sharding import PartitionSpec as P

MESH = pl.DeviceIdType.MESH
f32 = jnp.float32
bf16 = jnp.bfloat16

PAIRS = 4
HALF = 16
LEAVES = 8
SLOTS = 4
EMPTY = LEAVES * SLOTS


def split(value):
    high = value.astype(bf16)
    return high, (value - high.astype(f32)).astype(bf16)


def products(pieces, transposed):
    left, right = [], []
    for a_high, a_low, b_high, b_low in pieces:
        left += [a_high, a_high, a_low]
        right += [b_high, b_low, b_high]
    axis = 1 if transposed else 0
    return lax.dot_general(
        jnp.concatenate(left, axis=1), jnp.concatenate(right, axis=axis),
        (((1,), (axis,)), ((), ())), preferred_element_type=f32,
    )


def whole_kernel(
    targets, live, leaf_rhs, leaf_inverse, leaf_blocks, rhs_ref, top_ref, z_ref, own_ref,
    inverse, slots, slot_high, slot_low, y_high, y_low, u_ref, x_ref, x_high, x_low, top, top_high, top_low,
    pair_in, chip_sum, first_in, middle, second_in, plane_sum, y_in, update_out, update_in, rhs, solved,
    leaf_sem, inverse_sem, slots_sem, local_sem, blocks_s, blocks_r, rhs_s, rhs_r, pair_s, pair_r,
    first_s, first_r, second_s, second_r, y_s, y_r, update_s, update_r,
    spread_s, spread_r, chunk_s, chunk_r, line_s, line_r, swap_s, swap_r,
):
    row = lax.axis_index("row")
    col = lax.axis_index("col")
    core = lax.rem(row, 2)
    y = lax.div(row, 2)
    other = 1 - core
    z = lax.div(col, 4)
    x = lax.rem(col, 4)
    mate = {"row": 2 * y + other}

    def on_y(chip):
        return {"row": 2 * chip + core}

    def on_x(step):
        return {"col": 4 * z + lax.rem(x + step, 4)}

    def on_z(step):
        return {"col": 4 * lax.rem(z + step, 4) + x}

    def remote(src, dst, send, recv, device):
        return pltpu.make_async_remote_copy(
            src_ref=src, dst_ref=dst, send_sem=send, recv_sem=recv, device_id=device, device_id_type=MESH
        )

    barrier = pltpu.get_barrier_semaphore()
    pl.semaphore_signal(barrier, inc=1, device_id=mate, device_id_type=MESH)
    for step in range(1, PAIRS):
        pl.semaphore_signal(barrier, inc=1, device_id=on_y(lax.rem(y + step, PAIRS)), device_id_type=MESH)
    for step in range(1, 4):
        pl.semaphore_signal(barrier, inc=1, device_id=on_x(step), device_id_type=MESH)
        pl.semaphore_signal(barrier, inc=1, device_id=on_z(step), device_id_type=MESH)

    def leaf_copies(k):
        column = pl.ds(pl.multiple_of(k * 256, 256), 256)
        group = pl.ds(SLOTS * k, SLOTS)
        return (
            pltpu.make_async_copy(leaf_rhs.at[:, column], z_ref.at[k], leaf_sem.at[k]),
            pltpu.make_async_copy(leaf_inverse.at[k], inverse.at[k], inverse_sem.at[k]),
            pltpu.make_async_copy(leaf_blocks.at[group], slots.at[group], slots_sem.at[k]),
        )

    for k in range(LEAVES):
        for copy in leaf_copies(k):
            copy.start()
    local_copy = pltpu.make_async_copy(top_ref, top.at[core], local_sem)
    local_copy.start()
    rhs[core] = rhs_ref[core]
    zero_block = jnp.zeros((256, 256), bf16)
    slot_high[EMPTY] = zero_block
    slot_low[EMPTY] = zero_block

    pl.semaphore_wait(barrier, 10)
    blocks_copy = remote(top_ref, top.at[core], blocks_s, blocks_r, mate)
    blocks_copy.start()
    rhs_copy = remote(rhs_ref.at[other], rhs.at[core], rhs_s, rhs_r, mate)
    rhs_copy.start()

    @pl.loop(0, LEAVES)
    def _(k):
        for copy in leaf_copies(k):
            copy.wait()
        b_high, b_low = split(inverse[k])
        for part in range(2):
            rows = pl.ds(256 * part, 256)
            a_high, a_low = split(z_ref[k, rows])
            result = products([(a_high, a_low, b_high, b_low)], True)
            z_ref[k, rows] = result
            high, low = split(result)
            y_high[k, rows] = high
            y_low[k, rows] = low
        for j in range(SLOTS):
            high, low = split(slots[SLOTS * k + j])
            slot_high[SLOTS * k + j] = high
            slot_low[SLOTS * k + j] = low

    def place_of(k, level):
        place = jnp.int32(EMPTY)
        for j in range(SLOTS):
            used = jnp.logical_and(targets[k, j] == level, live[k] > j)
            place = jnp.where(used, SLOTS * k + j, place)
        return place

    def pair_copy(p):
        return remote(u_ref.at[p, :, :, :, other], pair_in.at[p], pair_s.at[p], pair_r.at[p], mate)

    def first_copy(p, level, step):
        if level == 0:
            src, device = chip_sum.at[p, 0, :, lax.rem(x + step, 4)], on_x(step)
        else:
            src, device = chip_sum.at[p, 1, lax.rem(z + step, 4)], on_z(step)
        return remote(
            src, first_in.at[p, level, step - 1], first_s.at[p, level, step - 1], first_r.at[p, level, step - 1], device
        )

    def second_copy(p, level, step):
        if level == 0:
            src, device = middle.at[p, 0, lax.rem(z + step, 4)], on_z(step)
        else:
            src, device = middle.at[p, 1, lax.rem(x + step, 4)], on_x(step)
        return remote(
            src, second_in.at[p, level, step - 1],
            second_s.at[p, level, step - 1], second_r.at[p, level, step - 1], device,
        )

    def y_copy(p, source):
        return remote(plane_sum.at[p], y_in.at[source], y_s.at[p], y_r.at[source], on_y(p))

    both = [(level, step) for step in (2, 1, 3) for level in range(2)]

    def update_copy(source, target):
        return remote(update_out.at[target], update_in.at[source], update_s.at[target], update_r.at[source], on_y(target))

    def top_parts(column, level):
        return top_high[column, level], top_low[column, level]

    def solve_forward():
        y_in[y] = jnp.zeros((2, HALF, 256), f32)
        for chip in range(PAIRS):

            @pl.when(y != chip)
            def _():
                y_copy(chip, chip).wait_recv()

        solved[...] = rhs[...] - plane_sum[y] - (y_in[0] + y_in[1] + y_in[2] + y_in[3])
        for chip in range(PAIRS - 1):

            @pl.when(y > chip)
            def _():
                update_copy(chip, y).wait_recv()
                solved[...] = solved[...] - update_in[chip]

        first = products([split(solved[0]) + top_parts(0, 2 * y)], True)
        first_parts = split(first)
        second = solved[1] - products([first_parts + top_parts(0, 2 * y + 1)], True)
        second = products([split(second) + top_parts(1, 2 * y + 1)], True)
        second_parts = split(second)
        solved[0] = first
        solved[1] = second
        for chip in range(1, PAIRS):

            @pl.when(y < chip)
            def _():
                for level in range(2):
                    update_out[chip, level] = products(
                        [
                            first_parts + top_parts(0, 2 * chip + level),
                            second_parts + top_parts(1, 2 * chip + level),
                        ],
                        True,
                    )
                update_copy(y, chip).start()

    @pl.loop(0, 33)
    def _(quarter):
        phase = lax.rem(quarter, 4)
        round_of = lax.div(quarter, 4)

        @pl.when(quarter < 16)
        def _():
            level = lax.rem(lax.div(quarter, 2), 2)
            part = lax.rem(quarter, 2)
            rows = pl.ds(pl.multiple_of(256 * part, 256), 256)
            pieces = []
            for k in range(LEAVES):
                place = place_of(k, 2 * round_of + level)
                pieces.append((y_high[k, rows], y_low[k, rows], slot_high[place], slot_low[place]))
            u_ref[round_of, level, pl.ds(2 * part, 2)] = products(pieces, True).reshape(2, 4, 2, HALF, 256)

            @pl.when(phase == 3)
            def _():
                pair_copy(round_of).start()

        @pl.when(jnp.logical_and(phase == 1, jnp.logical_and(quarter >= 5, quarter <= 17)))
        def _():
            p = round_of - 1
            pair_copy(p).wait_recv()
            chip_sum[p] = u_ref[p, :, :, :, core] + pair_in[p]
            for level, step in both:
                first_copy(p, level, step).start()

        @pl.when(quarter == 18)
        def _():
            rhs_copy.wait_recv()
            remote(top_ref, top.at[other], blocks_s, blocks_r, mate).wait_recv()
            local_copy.wait()
            for column in range(2):

                @pl.loop(0, 8)
                def _(level):
                    high, low = split(top[column, level])
                    top_high[column, level] = high
                    top_low[column, level] = low

        @pl.when(jnp.logical_and(phase == 0, jnp.logical_and(quarter >= 16, quarter <= 28)))
        def _():
            p = round_of - 4
            for level, step in both:
                second_copy(p, level, step).wait_recv()
            plane_sum[p, 0] = middle[p, 0, z] + second_in[p, 0, 0] + second_in[p, 0, 1] + second_in[p, 0, 2]
            plane_sum[p, 1] = middle[p, 1, x] + second_in[p, 1, 0] + second_in[p, 1, 1] + second_in[p, 1, 2]

            @pl.when(y != p)
            def _():
                y_copy(p, y).start()

        @pl.when(jnp.logical_and(phase == 0, jnp.logical_and(quarter >= 12, quarter <= 24)))
        def _():
            p = round_of - 3
            for level, step in both:
                first_copy(p, level, step).wait_recv()
            middle[p, 0] = chip_sum[p, 0, :, x] + first_in[p, 0, 0] + first_in[p, 0, 1] + first_in[p, 0, 2]
            middle[p, 1] = chip_sum[p, 1, z] + first_in[p, 1, 0] + first_in[p, 1, 1] + first_in[p, 1, 2]
            for level, step in both:
                second_copy(p, level, step).start()

        @pl.when(jnp.logical_and(phase == 0, y == round_of - 5))
        def _():
            solve_forward()

    def spread(p, step):
        chunk = x_ref.at[p, :, z, x, core]
        return remote(chunk, chunk, spread_s.at[step - 1], spread_r.at[p], on_y(lax.rem(y + step, PAIRS)))

    def solve_backward():
        second = products([split(solved[1]) + top_parts(1, 2 * y + 1)], False)
        first = solved[0] - products([split(second) + top_parts(0, 2 * y + 1)], False)
        first = products([split(first) + top_parts(0, 2 * y)], False)
        x_ref[y, 0, z, x, core] = first
        x_ref[y, 1, z, x, core] = second
        for step in range(1, PAIRS):
            spread(y, step).start()

    def chunk_copy(p, level, step):
        chunk = x_ref.at[p, level, z, x, core]
        device = on_z(step) if level == 0 else on_x(step)
        return remote(chunk, chunk, chunk_s.at[p, level, step - 1], chunk_r.at[p, level, step - 1], device)

    def line_copy(p, level, step):
        if level == 0:
            line, device = x_ref.at[p, 0, :, x, core], on_x(step)
        else:
            line, device = x_ref.at[p, 1, z, :, core], on_z(step)
        return remote(line, line, line_s.at[p, level, step - 1], line_r.at[p, level, step - 1], device)

    def send_lines(p):
        for level, step in both:
            chunk_copy(p, level, step).wait_recv()
        for level, step in both:
            line_copy(p, level, step).start()

    def swap_copy(p, half):
        part = x_ref.at[p, :, :, :, half]
        return remote(part, part, swap_s.at[p], swap_r.at[p], mate)

    def send_swap(p):
        for level, step in both:
            line_copy(p, level, step).wait_recv()
        swap_copy(p, core).start()

    def arrive(p):
        @pl.when(y != p)
        def _():
            spread(p, 1).wait_recv()

        @pl.when(y < p)
        def _():
            parts = [split(x_ref[p, level, z, x, core]) for level in range(2)]
            for column in range(2):
                solved[column] = solved[column] - products(
                    [parts[level] + top_parts(column, 2 * p + level) for level in range(2)], False
                )

        if p > 0:

            @pl.when(y == p - 1)
            def _():
                solve_backward()

        for level, step in both:
            chunk_copy(p, level, step).start()

    def take_swap(p):
        swap_copy(p, other).wait_recv()
        for level in range(2):
            high, low = split(x_ref[p, level].reshape(512, 256))
            x_high[level] = high
            x_low[level] = low

    def correct(p, begin, end):
        @pl.loop(begin, end)
        def _(k):
            places = [place_of(k, 2 * p + level) for level in range(2)]
            for part in range(2):
                rows = pl.ds(256 * part, 256)
                z_ref[k, rows] = z_ref[k, rows] - products(
                    [
                        (x_high[level, rows], x_low[level, rows], slot_high[places[level]], slot_low[places[level]])
                        for level in range(2)
                    ],
                    False,
                )

    @pl.when(y == PAIRS - 1)
    def _():
        solve_backward()

    arrive(3)
    send_lines(3)
    arrive(2)
    send_lines(2)
    send_swap(3)
    arrive(1)
    take_swap(3)
    correct(3, 0, 4)
    send_lines(1)
    correct(3, 4, 8)
    send_swap(2)
    arrive(0)
    take_swap(2)
    correct(2, 0, 4)
    send_lines(0)
    correct(2, 4, 8)
    send_swap(1)
    take_swap(1)
    correct(1, 0, 8)
    send_swap(0)
    take_swap(0)
    correct(0, 0, 8)
    own_ref[...] = x_ref[y, core, z, x]

    rhs_copy.wait_send()
    blocks_copy.wait_send()
    for p in range(PAIRS):
        pair_copy(p).wait_send()
        for level, step in both:
            first_copy(p, level, step).wait_send()
            second_copy(p, level, step).wait_send()
            chunk_copy(p, level, step).wait_send()
            line_copy(p, level, step).wait_send()
        swap_copy(p, core).wait_send()

        @pl.when(y != p)
        def _():
            y_copy(p, y).wait_send()

    for chip in range(1, PAIRS):

        @pl.when(y < chip)
        def _():
            update_copy(y, chip).wait_send()

    for step in range(1, PAIRS):
        spread(y, step).wait_send()


def whole_solve(targets, live, leaf_rhs, leaf_inverse, leaf_blocks, rhs, top_blocks):
    dma = pltpu.SemaphoreType.DMA
    vmem = pl.BlockSpec(memory_space=pltpu.VMEM)
    smem = pl.BlockSpec(memory_space=pltpu.SMEM)
    hbm = pl.BlockSpec(memory_space=pl.ANY)
    return pl.pallas_call(
        whole_kernel,
        out_shape=(
            jax.ShapeDtypeStruct((LEAVES, 512, 256), f32),
            jax.ShapeDtypeStruct((2, HALF, 256), f32),
        ),
        in_specs=[smem, smem, hbm, hbm, hbm, vmem, hbm],
        out_specs=(vmem, vmem),
        scratch_shapes=[
            pltpu.VMEM((LEAVES, 256, 256), f32),
            pltpu.VMEM((LEAVES * SLOTS, 256, 256), f32),
            pltpu.VMEM((LEAVES * SLOTS + 1, 256, 256), bf16),
            pltpu.VMEM((LEAVES * SLOTS + 1, 256, 256), bf16),
            pltpu.VMEM((LEAVES, 512, 256), bf16),
            pltpu.VMEM((LEAVES, 512, 256), bf16),
            pltpu.VMEM((PAIRS, 2, 4, 4, 2, HALF, 256), f32),
            pltpu.VMEM((PAIRS, 2, 4, 4, 2, HALF, 256), f32),
            pltpu.VMEM((2, 512, 256), bf16),
            pltpu.VMEM((2, 512, 256), bf16),
            pltpu.VMEM((2, 8, 256, 256), f32),
            pltpu.VMEM((2, 8, 256, 256), bf16),
            pltpu.VMEM((2, 8, 256, 256), bf16),
            pltpu.VMEM((PAIRS, 2, 4, 4, HALF, 256), f32),
            pltpu.VMEM((PAIRS, 2, 4, 4, HALF, 256), f32),
            pltpu.VMEM((PAIRS, 2, 3, 4, HALF, 256), f32),
            pltpu.VMEM((PAIRS, 2, 4, HALF, 256), f32),
            pltpu.VMEM((PAIRS, 2, 3, HALF, 256), f32),
            pltpu.VMEM((PAIRS, 2, HALF, 256), f32),
            pltpu.VMEM((PAIRS, 2, HALF, 256), f32),
            pltpu.VMEM((PAIRS, 2, HALF, 256), f32),
            pltpu.VMEM((PAIRS, 2, HALF, 256), f32),
            pltpu.VMEM((2, HALF, 256), f32),
            pltpu.VMEM((2, HALF, 256), f32),
            dma((LEAVES,)), dma((LEAVES,)), dma((LEAVES,)),
            dma,
            dma, dma, dma, dma,
            dma((PAIRS,)), dma((PAIRS,)),
            dma((PAIRS, 2, 3)), dma((PAIRS, 2, 3)),
            dma((PAIRS, 2, 3)), dma((PAIRS, 2, 3)),
            dma((PAIRS,)), dma((PAIRS,)),
            dma((PAIRS,)), dma((PAIRS,)),
            dma((PAIRS,)), dma((PAIRS,)),
            dma((PAIRS, 2, 3)), dma((PAIRS, 2, 3)),
            dma((PAIRS, 2, 3)), dma((PAIRS, 2, 3)),
            dma((PAIRS,)), dma((PAIRS,)),
        ],
        compiler_params=pltpu.CompilerParams(
            collective_id=0, has_side_effects=True, vmem_limit_bytes=60 * 1024 * 1024
        ),
        cost_estimate=pl.CostEstimate(flops=3 * 10**10, bytes_accessed=2 * 10**7, transcendentals=0),
    )(targets, live, leaf_rhs, leaf_inverse, leaf_blocks, rhs, top_blocks)


def last_kernel(z_ref, inverse_ref, out_ref):
    parts = split(inverse_ref[0])
    for part in range(2):
        rows = pl.ds(256 * part, 256)
        out_ref[rows] = products([split(z_ref[0, rows]) + parts], False)


def last_product(z, inverse):
    return pl.pallas_call(
        last_kernel,
        out_shape=jax.ShapeDtypeStruct((512, LEAVES * 256), f32),
        grid=(LEAVES,),
        in_specs=[
            pl.BlockSpec((1, 512, 256), lambda k: (k, 0, 0)),
            pl.BlockSpec((1, 256, 256), lambda k: (k, 0, 0)),
        ],
        out_specs=pl.BlockSpec((512, 256), lambda k: (0, k)),
        cost_estimate=pl.CostEstimate(flops=16 * 10**8, bytes_accessed=10**7, transcendentals=0),
    )(z, inverse)


def on_device(leaf_rhs, top_rhs, leaf_inverse, leaf_blocks, leaf_targets, leaf_live, top_blocks):
    z, own = whole_solve(
        leaf_targets, leaf_live, leaf_rhs, leaf_inverse, leaf_blocks.reshape(LEAVES * SLOTS, 256, 256),
        top_rhs.reshape(2, HALF, 256), top_blocks[0],
    )
    return (last_product(z, leaf_inverse), own.reshape(2 * HALF, 256))


def solution(mesh):
    in_specs = (
        P(None, ("row", "col")),
        P("col", "row"),
        P(("row", "col"), None, None),
        P(("row", "col"), None, None, None),
        P(("row", "col"), None),
        P(("row", "col")),
        P("row", None, None, None),
    )
    out_specs = (P(None, ("row", "col")), P("col", "row"))
    return jax.shard_map(
        on_device, mesh=mesh, in_specs=in_specs, out_specs=out_specs, check_vma=False
    )
```

```python
import jax
import jax.numpy as jnp
from jax import lax
from jax.experimental import pallas as pl
from jax.experimental.pallas import tpu as pltpu
from jax.sharding import PartitionSpec as P

MESH = pl.DeviceIdType.MESH
f32 = jnp.float32
bf16 = jnp.bfloat16

PAIRS = 4
HALF = 16
LEAVES = 8
SLOTS = 4
GROUP = 8
EMPTY = LEAVES * SLOTS


def split(value):
    high = value.astype(bf16)
    return high, (value - high.astype(f32)).astype(bf16)


def products(pieces, transposed):
    left, right = [], []
    for a_high, a_low, b_high, b_low in pieces:
        left += [a_high, a_high, a_low]
        right += [b_high, b_low, b_high]
    axis = 1 if transposed else 0
    return lax.dot_general(
        jnp.concatenate(left, axis=1), jnp.concatenate(right, axis=axis),
        (((1,), (axis,)), ((), ())), preferred_element_type=f32,
    )


def whole_kernel(
    targets_ref, live_ref, leaf_rhs, leaf_inverse, leaf_blocks, rhs_ref, top_ref, z_out, own_out,
    targets, live, z_ref, inverse, slots, slot_high, slot_low, y_high, y_low, u_ref, x_ref, x_high, x_low, top, top_high, top_low,
    pair_in, chip_sum, first_in, middle, second_in, plane_sum, y_in, update_out, update_in, rhs, solved,
    leaf_sem, inverse_sem, slots_sem, out_sem, local_sem, index_sem, own_sem, blocks_s, blocks_r, rhs_s, rhs_r, pair_s, pair_r,
    first_s, first_r, second_s, second_r, y_s, y_r, update_s, update_r,
    spread_s, spread_r, chunk_s, chunk_r, line_s, line_r, swap_s, swap_r,
):
    row = lax.axis_index("row")
    col = lax.axis_index("col")
    core = lax.rem(row, 2)
    y = lax.div(row, 2)
    other = 1 - core
    z = lax.div(col, 4)
    x = lax.rem(col, 4)
    mate = {"row": 2 * y + other}

    def on_y(chip):
        return {"row": 2 * chip + core}

    def on_x(step):
        return {"col": 4 * z + lax.rem(x + step, 4)}

    def on_z(step):
        return {"col": 4 * lax.rem(z + step, 4) + x}

    def remote(src, dst, send, recv, device):
        return pltpu.make_async_remote_copy(
            src_ref=src, dst_ref=dst, send_sem=send, recv_sem=recv, device_id=device, device_id_type=MESH
        )

    barrier = pltpu.get_barrier_semaphore()
    pl.semaphore_signal(barrier, inc=1, device_id=mate, device_id_type=MESH)
    for step in range(1, PAIRS):
        pl.semaphore_signal(barrier, inc=1, device_id=on_y(lax.rem(y + step, PAIRS)), device_id_type=MESH)
    for step in range(1, 4):
        pl.semaphore_signal(barrier, inc=1, device_id=on_x(step), device_id_type=MESH)
        pl.semaphore_signal(barrier, inc=1, device_id=on_z(step), device_id_type=MESH)

    def leaf_copies(k):
        column = pl.ds(pl.multiple_of(k * 256, 256), 256)
        group = pl.ds(SLOTS * k, SLOTS)
        return (
            pltpu.make_async_copy(leaf_rhs.at[:, :, :, column], z_ref.at[k], leaf_sem.at[k]),
            pltpu.make_async_copy(leaf_inverse.at[k], inverse.at[k], inverse_sem.at[k]),
            pltpu.make_async_copy(leaf_blocks.at[group], slots.at[group], slots_sem.at[k]),
        )

    index_copies = (
        pltpu.make_async_copy(targets_ref, targets, index_sem.at[0]),
        pltpu.make_async_copy(live_ref, live, index_sem.at[1]),
    )
    for copy in index_copies:
        copy.start()
    for k in range(LEAVES):
        for copy in leaf_copies(k):
            copy.start()
    local_copies = (
        pltpu.make_async_copy(top_ref, top.at[core], local_sem.at[0]),
        pltpu.make_async_copy(rhs_ref.at[core], rhs.at[core], local_sem.at[1]),
    )
    for copy in local_copies:
        copy.start()
    own_copy = pltpu.make_async_copy(x_ref.at[y, core, z, x], own_out, own_sem)
    zero_block = jnp.zeros((256, 256), bf16)
    slot_high[EMPTY] = zero_block
    slot_low[EMPTY] = zero_block

    @pl.loop(0, LEAVES)
    def _(k):
        for copy in leaf_copies(k):
            copy.wait()
        b_high, b_low = split(inverse[k])
        for part in range(2):
            rows = pl.ds(256 * part, 256)
            groups = pl.ds(8 * part, 8)
            a_high, a_low = split(z_ref[k, groups].reshape(256, 256))
            result = products([(a_high, a_low, b_high, b_low)], True)
            z_ref[k, groups] = result.reshape(8, 2, HALF, 256)
            high, low = split(result)
            y_high[k, rows] = high
            y_low[k, rows] = low
        for j in range(SLOTS):
            high, low = split(slots[SLOTS * k + j])
            slot_high[SLOTS * k + j] = high
            slot_low[SLOTS * k + j] = low

    for copy in index_copies:
        copy.wait()
    pl.semaphore_wait(barrier, 10)
    blocks_copy = remote(top_ref, top.at[core], blocks_s, blocks_r, mate)
    blocks_copy.start()
    rhs_copy = remote(rhs_ref.at[other], rhs.at[core], rhs_s, rhs_r, mate)
    rhs_copy.start()

    def place_of(k, level):
        place = jnp.int32(EMPTY)
        for j in range(SLOTS):
            used = jnp.logical_and(targets[j, k] == level, live[k] > j)
            place = jnp.where(used, SLOTS * k + j, place)
        return place

    def pair_copy(p):
        return remote(u_ref.at[p, :, :, :, other], pair_in.at[p], pair_s.at[p], pair_r.at[p], mate)

    def first_copy(p, level, step):
        if level == 0:
            src, device = chip_sum.at[p, 0, :, lax.rem(x + step, 4)], on_x(step)
        else:
            src, device = chip_sum.at[p, 1, lax.rem(z + step, 4)], on_z(step)
        return remote(
            src, first_in.at[p, level, step - 1], first_s.at[p, level, step - 1], first_r.at[p, level, step - 1], device
        )

    def second_copy(p, level, step):
        if level == 0:
            src, device = middle.at[p, 0, lax.rem(z + step, 4)], on_z(step)
        else:
            src, device = middle.at[p, 1, lax.rem(x + step, 4)], on_x(step)
        return remote(
            src, second_in.at[p, level, step - 1],
            second_s.at[p, level, step - 1], second_r.at[p, level, step - 1], device,
        )

    def y_copy(p, source):
        return remote(plane_sum.at[p], y_in.at[source], y_s.at[p], y_r.at[source], on_y(p))

    both = [(level, step) for step in (2, 1, 3) for level in range(2)]

    def update_copy(source, target):
        return remote(update_out.at[target], update_in.at[source], update_s.at[target], update_r.at[source], on_y(target))

    def top_parts(column, level):
        return top_high[column, level], top_low[column, level]

    def solve_forward():
        y_in[y] = jnp.zeros((2, HALF, 256), f32)
        for chip in range(PAIRS):

            @pl.when(y != chip)
            def _():
                y_copy(chip, chip).wait_recv()

        solved[...] = rhs[...] - plane_sum[y] - (y_in[0] + y_in[1] + y_in[2] + y_in[3])
        for chip in range(PAIRS - 1):

            @pl.when(y > chip)
            def _():
                update_copy(chip, y).wait_recv()
                solved[...] = solved[...] - update_in[chip]

        first = products([split(solved[0]) + top_parts(0, 2 * y)], True)
        first_parts = split(first)
        second = solved[1] - products([first_parts + top_parts(0, 2 * y + 1)], True)
        second = products([split(second) + top_parts(1, 2 * y + 1)], True)
        second_parts = split(second)
        solved[0] = first
        solved[1] = second

        def update(chip):
            for level in range(2):
                update_out[chip, level] = products(
                    [
                        first_parts + top_parts(0, 2 * chip + level),
                        second_parts + top_parts(1, 2 * chip + level),
                    ],
                    True,
                )

        update(lax.rem(y + 1, PAIRS))

        @pl.when(y < PAIRS - 1)
        def _():
            update_copy(y, lax.rem(y + 1, PAIRS)).start()

        for chip in range(2, PAIRS):

            @pl.when(y < chip - 1)
            def _():
                update(chip)
                update_copy(y, chip).start()

    @pl.loop(0, 32)
    def _(quarter):
        phase = lax.rem(quarter, 4)
        round_of = lax.div(quarter, 4)

        @pl.when(quarter < 16)
        def _():
            level = lax.rem(lax.div(quarter, 2), 2)
            part = lax.rem(quarter, 2)
            rows = pl.ds(pl.multiple_of(256 * part, 256), 256)
            pieces = []
            for k in range(LEAVES):
                place = place_of(k, 2 * round_of + level)
                pieces.append((y_high[k, rows], y_low[k, rows], slot_high[place], slot_low[place]))
            u_ref[round_of, level, pl.ds(2 * part, 2)] = products(pieces, True).reshape(2, 4, 2, HALF, 256)

            @pl.when(phase == 3)
            def _():
                pair_copy(round_of).start()

        @pl.when(jnp.logical_and(phase == 0, jnp.logical_and(quarter >= 4, quarter <= 16)))
        def _():
            p = round_of - 1
            pair_copy(p).wait_recv()
            chip_sum[p] = u_ref[p, :, :, :, core] + pair_in[p]
            for level, step in both:
                first_copy(p, level, step).start()

        @pl.when(quarter == 18)
        def _():
            rhs_copy.wait_recv()
            remote(top_ref, top.at[other], blocks_s, blocks_r, mate).wait_recv()
            for copy in local_copies:
                copy.wait()
            for column in range(2):

                @pl.loop(0, 8)
                def _(level):
                    high, low = split(top[column, level])
                    top_high[column, level] = high
                    top_low[column, level] = low

        @pl.when(jnp.logical_and(phase == 3, jnp.logical_and(quarter >= 15, quarter <= 27)))
        def _():
            p = round_of - 3
            for level, step in both:
                second_copy(p, level, step).wait_recv()
            plane_sum[p, 0] = middle[p, 0, z] + second_in[p, 0, 0] + second_in[p, 0, 1] + second_in[p, 0, 2]
            plane_sum[p, 1] = middle[p, 1, x] + second_in[p, 1, 0] + second_in[p, 1, 1] + second_in[p, 1, 2]

            @pl.when(y != p)
            def _():
                y_copy(p, y).start()

        @pl.when(jnp.logical_and(phase == 3, jnp.logical_and(quarter >= 11, quarter <= 23)))
        def _():
            p = round_of - 2
            for level, step in both:
                first_copy(p, level, step).wait_recv()
            middle[p, 0] = chip_sum[p, 0, :, x] + first_in[p, 0, 0] + first_in[p, 0, 1] + first_in[p, 0, 2]
            middle[p, 1] = chip_sum[p, 1, z] + first_in[p, 1, 0] + first_in[p, 1, 1] + first_in[p, 1, 2]
            for level, step in both:
                second_copy(p, level, step).start()

        @pl.when(jnp.logical_and(phase == 3, y == round_of - 4))
        def _():
            solve_forward()

    def spread(p, step):
        chunk = x_ref.at[p, :, z, x, core]
        return remote(chunk, chunk, spread_s.at[step - 1], spread_r.at[p], on_y(lax.rem(y + step, PAIRS)))

    def solve_backward(first, second):
        second = products([split(second) + top_parts(1, 2 * y + 1)], False)
        first = first - products([split(second) + top_parts(0, 2 * y + 1)], False)
        first = products([split(first) + top_parts(0, 2 * y)], False)
        x_ref[y, 0, z, x, core] = first
        x_ref[y, 1, z, x, core] = second
        for step in range(1, PAIRS):
            spread(y, step).start()

    def chunk_copy(p, level, step):
        chunk = x_ref.at[p, level, z, x, core]
        device = on_z(step) if level == 0 else on_x(step)
        return remote(chunk, chunk, chunk_s.at[p, level, step - 1], chunk_r.at[p, level, step - 1], device)

    def line_copy(p, level, step):
        if level == 0:
            line, device = x_ref.at[p, 0, :, x, core], on_x(step)
        else:
            line, device = x_ref.at[p, 1, z, :, core], on_z(step)
        return remote(line, line, line_s.at[p, level, step - 1], line_r.at[p, level, step - 1], device)

    def send_lines(p):
        for level, step in both:
            chunk_copy(p, level, step).wait_recv()
        for level, step in both:
            line_copy(p, level, step).start()

    def swap_copy(p, half):
        part = x_ref.at[p, :, :, :, half]
        return remote(part, part, swap_s.at[p], swap_r.at[p], mate)

    def send_swap(p):
        for level, step in both:
            line_copy(p, level, step).wait_recv()
        swap_copy(p, core).start()

    def arrive(p):
        @pl.when(y != p)
        def _():
            spread(p, 1).wait_recv()

        def subtract():
            parts = [split(x_ref[p, level, z, x, core]) for level in range(2)]
            return [
                solved[column]
                - products([parts[level] + top_parts(column, 2 * p + level) for level in range(2)], False)
                for column in range(2)
            ]

        if p > 0:

            @pl.when(y == p - 1)
            def _():
                solve_backward(*subtract())

        if p > 1:

            @pl.when(y < p - 1)
            def _():
                solved[0], solved[1] = subtract()

        for level, step in both:
            chunk_copy(p, level, step).start()

    def take(p, half):
        for level in range(2):
            high, low = split(x_ref[p, level, :, :, half].reshape(256, 256))
            x_high[level] = high
            x_low[level] = low

    def out_copy(k):
        return pltpu.make_async_copy(z_ref.at[k], z_out.at[k], out_sem.at[k])

    def correct(p, half, leave=False):
        @pl.loop(0, LEAVES // GROUP)
        def _(group):
            for k in [GROUP * group + i for i in range(GROUP)]:
                pieces = []
                for level in range(2):
                    place = place_of(k, 2 * p + level)
                    pieces.append((x_high[level], x_low[level], slot_high[place], slot_low[place]))
                part = z_ref[k, :, half].reshape(256, 256) - products(pieces, False)
                z_ref[k, :, half] = part.reshape(16, HALF, 256)
                if leave:
                    out_copy(k).start()

    def own_half(p):
        take(p, core)
        correct(p, core)

    def other_half(p):
        swap_copy(p, other).wait_recv()
        if p == 0:
            own_copy.start()
        take(p, other)
        correct(p, other, leave=p == 0)

    @pl.when(y == PAIRS - 1)
    def _():
        solve_backward(solved[0], solved[1])

    arrive(3)
    send_lines(3)
    arrive(2)
    send_lines(2)
    send_swap(3)
    arrive(1)
    own_half(3)
    send_lines(1)
    send_swap(2)
    arrive(0)
    other_half(3)
    own_half(2)
    send_lines(0)
    send_swap(1)
    other_half(2)
    own_half(1)
    other_half(1)
    send_swap(0)
    own_half(0)
    other_half(0)

    own_copy.wait()
    for k in range(LEAVES):
        out_copy(k).wait()
    rhs_copy.wait_send()
    blocks_copy.wait_send()
    for p in range(PAIRS):
        pair_copy(p).wait_send()
        for level, step in both:
            first_copy(p, level, step).wait_send()
            second_copy(p, level, step).wait_send()
            chunk_copy(p, level, step).wait_send()
            line_copy(p, level, step).wait_send()
        swap_copy(p, core).wait_send()

        @pl.when(y != p)
        def _():
            y_copy(p, y).wait_send()

    for chip in range(1, PAIRS):

        @pl.when(y < chip)
        def _():
            update_copy(y, chip).wait_send()

    for step in range(1, PAIRS):
        spread(y, step).wait_send()


def whole_solve(targets, live, leaf_rhs, leaf_inverse, leaf_blocks, rhs, top_blocks):
    dma = pltpu.SemaphoreType.DMA
    hbm = pl.BlockSpec(memory_space=pl.ANY)
    return pl.pallas_call(
        whole_kernel,
        out_shape=(
            jax.ShapeDtypeStruct((LEAVES, 16, 2, HALF, 256), f32),
            jax.ShapeDtypeStruct((2, HALF, 256), f32),
        ),
        in_specs=[hbm] * 7,
        out_specs=(hbm, hbm),
        scratch_shapes=[
            pltpu.SMEM((SLOTS, LEAVES), jnp.int32),
            pltpu.SMEM((LEAVES,), jnp.int32),
            pltpu.VMEM((LEAVES, 16, 2, HALF, 256), f32),
            pltpu.VMEM((LEAVES, 256, 256), f32),
            pltpu.VMEM((LEAVES * SLOTS, 256, 256), f32),
            pltpu.VMEM((LEAVES * SLOTS + 1, 256, 256), bf16),
            pltpu.VMEM((LEAVES * SLOTS + 1, 256, 256), bf16),
            pltpu.VMEM((LEAVES, 512, 256), bf16),
            pltpu.VMEM((LEAVES, 512, 256), bf16),
            pltpu.VMEM((PAIRS, 2, 4, 4, 2, HALF, 256), f32),
            pltpu.VMEM((PAIRS, 2, 4, 4, 2, HALF, 256), f32),
            pltpu.VMEM((2, 256, 256), bf16),
            pltpu.VMEM((2, 256, 256), bf16),
            pltpu.VMEM((2, 8, 256, 256), f32),
            pltpu.VMEM((2, 8, 256, 256), bf16),
            pltpu.VMEM((2, 8, 256, 256), bf16),
            pltpu.VMEM((PAIRS, 2, 4, 4, HALF, 256), f32),
            pltpu.VMEM((PAIRS, 2, 4, 4, HALF, 256), f32),
            pltpu.VMEM((PAIRS, 2, 3, 4, HALF, 256), f32),
            pltpu.VMEM((PAIRS, 2, 4, HALF, 256), f32),
            pltpu.VMEM((PAIRS, 2, 3, HALF, 256), f32),
            pltpu.VMEM((PAIRS, 2, HALF, 256), f32),
            pltpu.VMEM((PAIRS, 2, HALF, 256), f32),
            pltpu.VMEM((PAIRS, 2, HALF, 256), f32),
            pltpu.VMEM((PAIRS, 2, HALF, 256), f32),
            pltpu.VMEM((2, HALF, 256), f32),
            pltpu.VMEM((2, HALF, 256), f32),
            dma((LEAVES,)), dma((LEAVES,)), dma((LEAVES,)), dma((LEAVES,)),
            dma((2,)), dma((2,)), dma,
            dma, dma, dma, dma,
            dma((PAIRS,)), dma((PAIRS,)),
            dma((PAIRS, 2, 3)), dma((PAIRS, 2, 3)),
            dma((PAIRS, 2, 3)), dma((PAIRS, 2, 3)),
            dma((PAIRS,)), dma((PAIRS,)),
            dma((PAIRS,)), dma((PAIRS,)),
            dma((PAIRS,)), dma((PAIRS,)),
            dma((PAIRS, 2, 3)), dma((PAIRS, 2, 3)),
            dma((PAIRS, 2, 3)), dma((PAIRS, 2, 3)),
            dma((PAIRS,)), dma((PAIRS,)),
        ],
        compiler_params=pltpu.CompilerParams(
            collective_id=0, has_side_effects=True, vmem_limit_bytes=60 * 1024 * 1024
        ),
        cost_estimate=pl.CostEstimate(flops=3 * 10**10, bytes_accessed=2 * 10**7, transcendentals=0),
    )(targets, live, leaf_rhs, leaf_inverse, leaf_blocks, rhs, top_blocks)


def last_kernel(z_hbm, inverse_hbm, out_hbm, z_ref, inverse_ref, out_ref, z_sem, inverse_sem, out_sem):
    def copies(k):
        return (
            pltpu.make_async_copy(z_hbm.at[k], z_ref.at[k], z_sem.at[k]),
            pltpu.make_async_copy(inverse_hbm.at[k], inverse_ref.at[k], inverse_sem.at[k]),
        )

    def out_copy(k):
        column = pl.ds(pl.multiple_of(k * 256, 256), 256)
        return pltpu.make_async_copy(out_ref.at[k], out_hbm.at[:, column], out_sem.at[k])

    for k in range(LEAVES):
        for copy in copies(k):
            copy.start()

    @pl.loop(0, LEAVES)
    def _(k):
        for copy in copies(k):
            copy.wait()
        parts = split(inverse_ref[k])
        for part in range(2):
            rows = pl.ds(256 * part, 256)
            out_ref[k, rows] = products([split(z_ref[k, rows]) + parts], False)
        out_copy(k).start()

    for k in range(LEAVES):
        out_copy(k).wait()


def last_product(z, inverse):
    hbm = pl.BlockSpec(memory_space=pl.ANY)
    dma = pltpu.SemaphoreType.DMA
    return pl.pallas_call(
        last_kernel,
        out_shape=jax.ShapeDtypeStruct((512, LEAVES * 256), f32),
        in_specs=[hbm, hbm],
        out_specs=hbm,
        scratch_shapes=[
            pltpu.VMEM((LEAVES, 512, 256), f32),
            pltpu.VMEM((LEAVES, 256, 256), f32),
            pltpu.VMEM((LEAVES, 512, 256), f32),
            dma((LEAVES,)), dma((LEAVES,)), dma((LEAVES,)),
        ],
        compiler_params=pltpu.CompilerParams(vmem_limit_bytes=60 * 1024 * 1024),
        cost_estimate=pl.CostEstimate(flops=16 * 10**8, bytes_accessed=10**7, transcendentals=0),
    )(z, inverse)


def on_device(leaf_rhs, top_rhs, leaf_inverse, leaf_blocks, leaf_targets, leaf_live, top_blocks):
    z, own = whole_solve(
        leaf_targets.T, leaf_live, leaf_rhs.reshape(16, 2, HALF, LEAVES * 256), leaf_inverse, leaf_blocks.reshape(LEAVES * SLOTS, 256, 256),
        top_rhs.reshape(2, HALF, 256), top_blocks[0],
    )
    return (last_product(z.reshape(LEAVES, 512, 256), leaf_inverse), own.reshape(2 * HALF, 256))


def solution(mesh):
    in_specs = (
        P(None, ("row", "col")),
        P("col", "row"),
        P(("row", "col"), None, None),
        P(("row", "col"), None, None, None),
        P(("row", "col"), None),
        P(("row", "col")),
        P("row", None, None, None),
    )
    out_specs = (P(None, ("row", "col")), P("col", "row"))
    return jax.shard_map(
        on_device, mesh=mesh, in_specs=in_specs, out_specs=out_specs, check_vma=False
    )
```

```python
import jax
import jax.numpy as jnp
from jax import lax
from jax.experimental import pallas as pl
from jax.experimental.pallas import tpu as pltpu
from jax.sharding import PartitionSpec as P

MESH = pl.DeviceIdType.MESH
f32 = jnp.float32
bf16 = jnp.bfloat16

PAIRS = 4
HALF = 16
LEAVES = 8
SLOTS = 4
GROUP = 8
EMPTY = LEAVES * SLOTS


def split(value):
    high = value.astype(bf16)
    return high, (value - high.astype(f32)).astype(bf16)


def products(pieces, transposed):
    left, right = [], []
    for a_high, a_low, b_high, b_low in pieces:
        left += [a_high, a_high, a_low]
        right += [b_high, b_low, b_high]
    axis = 1 if transposed else 0
    return lax.dot_general(
        jnp.concatenate(left, axis=1), jnp.concatenate(right, axis=axis),
        (((1,), (axis,)), ((), ())), preferred_element_type=f32,
    )


def small_products(pieces, transposed):
    axis = 1 if transposed else 0
    dims = (((1,), (axis,)), ((), ()))
    high = jnp.concatenate([piece[0] for piece in pieces], axis=1)
    both = jnp.concatenate([high, jnp.concatenate([piece[1] for piece in pieces], axis=1)], axis=0)
    b_high = jnp.concatenate([piece[2] for piece in pieces], axis=axis)
    b_low = jnp.concatenate([piece[3] for piece in pieces], axis=axis)
    upper = lax.dot_general(both, b_high, dims, preferred_element_type=f32)
    lower = lax.dot_general(high, b_low, dims, preferred_element_type=f32)
    return upper[:HALF] + upper[HALF:] + lower


def whole_kernel(
    targets_ref, live_ref, leaf_rhs, leaf_inverse, leaf_blocks, rhs_ref, top_ref, z_out, own_out,
    targets, live, z_ref, inverse, slots, slot_high, slot_low, y_high, y_low, u_ref, x_ref, x_high, x_low, top, top_high, top_low,
    pair_in, chip_sum, first_in, middle, second_in, plane_sum, y_in, update_out, update_in, rhs, solved,
    leaf_sem, inverse_sem, slots_sem, out_sem, local_sem, index_sem, own_sem, blocks_s, blocks_r, rhs_s, rhs_r, pair_s, pair_r,
    first_s, first_r, second_s, second_r, y_s, y_r, update_s, update_r,
    spread_s, spread_r, chunk_s, chunk_r, line_s, line_r, swap_s, swap_r,
):
    row = lax.axis_index("row")
    col = lax.axis_index("col")
    core = lax.rem(row, 2)
    y = lax.div(row, 2)
    other = 1 - core
    z = lax.div(col, 4)
    x = lax.rem(col, 4)
    mate = {"row": 2 * y + other}

    def on_y(chip):
        return {"row": 2 * chip + core}

    def on_x(step):
        return {"col": 4 * z + lax.rem(x + step, 4)}

    def on_z(step):
        return {"col": 4 * lax.rem(z + step, 4) + x}

    def remote(src, dst, send, recv, device):
        return pltpu.make_async_remote_copy(
            src_ref=src, dst_ref=dst, send_sem=send, recv_sem=recv, device_id=device, device_id_type=MESH
        )

    barrier = pltpu.get_barrier_semaphore()
    pl.semaphore_signal(barrier, inc=1, device_id=mate, device_id_type=MESH)
    for step in range(1, PAIRS):
        pl.semaphore_signal(barrier, inc=1, device_id=on_y(lax.rem(y + step, PAIRS)), device_id_type=MESH)
    for step in range(1, 4):
        pl.semaphore_signal(barrier, inc=1, device_id=on_x(step), device_id_type=MESH)
        pl.semaphore_signal(barrier, inc=1, device_id=on_z(step), device_id_type=MESH)

    def leaf_copies(k):
        column = pl.ds(pl.multiple_of(k * 256, 256), 256)
        group = pl.ds(SLOTS * k, SLOTS)
        return (
            pltpu.make_async_copy(leaf_rhs.at[:, :, :, column], z_ref.at[k], leaf_sem.at[k]),
            pltpu.make_async_copy(leaf_inverse.at[k], inverse.at[k], inverse_sem.at[k]),
            pltpu.make_async_copy(leaf_blocks.at[group], slots.at[group], slots_sem.at[k]),
        )

    index_copies = (
        pltpu.make_async_copy(targets_ref, targets, index_sem.at[0]),
        pltpu.make_async_copy(live_ref, live, index_sem.at[1]),
    )
    for copy in index_copies:
        copy.start()
    for k in range(LEAVES):
        for copy in leaf_copies(k):
            copy.start()
    local_copies = (
        pltpu.make_async_copy(top_ref, top.at[core], local_sem.at[0]),
        pltpu.make_async_copy(rhs_ref.at[core], rhs.at[core], local_sem.at[1]),
    )
    for copy in local_copies:
        copy.start()
    own_copy = pltpu.make_async_copy(x_ref.at[y, core, z, x], own_out, own_sem)
    zero_block = jnp.zeros((256, 256), bf16)
    slot_high[EMPTY] = zero_block
    slot_low[EMPTY] = zero_block

    @pl.loop(0, LEAVES)
    def _(k):
        for copy in leaf_copies(k):
            copy.wait()
        b_high, b_low = split(inverse[k])
        for part in range(2):
            rows = pl.ds(256 * part, 256)
            groups = pl.ds(8 * part, 8)
            a_high, a_low = split(z_ref[k, groups].reshape(256, 256))
            result = products([(a_high, a_low, b_high, b_low)], True)
            z_ref[k, groups] = result.reshape(8, 2, HALF, 256)
            high, low = split(result)
            y_high[k, rows] = high
            y_low[k, rows] = low
        for j in range(SLOTS):
            high, low = split(slots[SLOTS * k + j])
            slot_high[SLOTS * k + j] = high
            slot_low[SLOTS * k + j] = low

    for copy in index_copies:
        copy.wait()
    pl.semaphore_wait(barrier, 10)
    blocks_copy = remote(top_ref, top.at[core], blocks_s, blocks_r, mate)
    blocks_copy.start()
    rhs_copy = remote(rhs_ref.at[other], rhs.at[core], rhs_s, rhs_r, mate)
    rhs_copy.start()

    def place_of(k, level):
        place = jnp.int32(EMPTY)
        for j in range(SLOTS):
            used = jnp.logical_and(targets[j, k] == level, live[k] > j)
            place = jnp.where(used, SLOTS * k + j, place)
        return place

    def pair_copy(p):
        return remote(u_ref.at[p, :, :, :, other], pair_in.at[p], pair_s.at[p], pair_r.at[p], mate)

    def first_copy(p, level, step):
        if level == 0:
            src, device = chip_sum.at[p, 0, :, lax.rem(x + step, 4)], on_x(step)
        else:
            src, device = chip_sum.at[p, 1, lax.rem(z + step, 4)], on_z(step)
        return remote(
            src, first_in.at[p, level, step - 1], first_s.at[p, level, step - 1], first_r.at[p, level, step - 1], device
        )

    def second_copy(p, level, step):
        if level == 0:
            src, device = middle.at[p, 0, lax.rem(z + step, 4)], on_z(step)
        else:
            src, device = middle.at[p, 1, lax.rem(x + step, 4)], on_x(step)
        return remote(
            src, second_in.at[p, level, step - 1],
            second_s.at[p, level, step - 1], second_r.at[p, level, step - 1], device,
        )

    def y_copy(p, source):
        return remote(plane_sum.at[p], y_in.at[source], y_s.at[p], y_r.at[source], on_y(p))

    both = [(level, step) for step in (2, 1, 3) for level in range(2)]

    def update_copy(source, target):
        return remote(update_out.at[target], update_in.at[source], update_s.at[target], update_r.at[source], on_y(target))

    def top_parts(column, level):
        return top_high[column, level], top_low[column, level]

    def solve_forward():
        y_in[y] = jnp.zeros((2, HALF, 256), f32)
        for chip in range(PAIRS):

            @pl.when(y != chip)
            def _():
                y_copy(chip, chip).wait_recv()

        solved[...] = rhs[...] - plane_sum[y] - (y_in[0] + y_in[1] + y_in[2] + y_in[3])
        for chip in range(PAIRS - 1):

            @pl.when(y > chip)
            def _():
                update_copy(chip, y).wait_recv()
                solved[...] = solved[...] - update_in[chip]

        first = small_products([split(solved[0]) + top_parts(0, 2 * y)], True)
        first_parts = split(first)
        second = solved[1] - small_products([first_parts + top_parts(0, 2 * y + 1)], True)
        second = small_products([split(second) + top_parts(1, 2 * y + 1)], True)
        second_parts = split(second)
        solved[0] = first
        solved[1] = second

        def update(chip):
            for level in range(2):
                update_out[chip, level] = small_products(
                    [
                        first_parts + top_parts(0, 2 * chip + level),
                        second_parts + top_parts(1, 2 * chip + level),
                    ],
                    True,
                )

        update(lax.rem(y + 1, PAIRS))

        @pl.when(y < PAIRS - 1)
        def _():
            update_copy(y, lax.rem(y + 1, PAIRS)).start()

        for chip in range(2, PAIRS):

            @pl.when(y < chip - 1)
            def _():
                update(chip)
                update_copy(y, chip).start()

    @pl.loop(0, 32)
    def _(quarter):
        phase = lax.rem(quarter, 4)
        round_of = lax.div(quarter, 4)

        @pl.when(quarter < 16)
        def _():
            level = lax.rem(lax.div(quarter, 2), 2)
            part = lax.rem(quarter, 2)
            rows = pl.ds(pl.multiple_of(256 * part, 256), 256)
            pieces = []
            for k in range(LEAVES):
                place = place_of(k, 2 * round_of + level)
                pieces.append((y_high[k, rows], y_low[k, rows], slot_high[place], slot_low[place]))
            u_ref[round_of, level, pl.ds(2 * part, 2)] = products(pieces, True).reshape(2, 4, 2, HALF, 256)

            @pl.when(phase == 3)
            def _():
                pair_copy(round_of).start()

        @pl.when(jnp.logical_and(phase == 0, jnp.logical_and(quarter >= 4, quarter <= 16)))
        def _():
            p = round_of - 1
            pair_copy(p).wait_recv()
            chip_sum[p] = u_ref[p, :, :, :, core] + pair_in[p]
            for level, step in both:
                first_copy(p, level, step).start()

        @pl.when(quarter == 18)
        def _():
            rhs_copy.wait_recv()
            remote(top_ref, top.at[other], blocks_s, blocks_r, mate).wait_recv()
            for copy in local_copies:
                copy.wait()
            for column in range(2):

                @pl.loop(0, 8)
                def _(level):
                    high, low = split(top[column, level])
                    top_high[column, level] = high
                    top_low[column, level] = low

        @pl.when(jnp.logical_and(phase == 3, jnp.logical_and(quarter >= 15, quarter <= 27)))
        def _():
            p = round_of - 3
            for level, step in both:
                second_copy(p, level, step).wait_recv()
            plane_sum[p, 0] = middle[p, 0, z] + second_in[p, 0, 0] + second_in[p, 0, 1] + second_in[p, 0, 2]
            plane_sum[p, 1] = middle[p, 1, x] + second_in[p, 1, 0] + second_in[p, 1, 1] + second_in[p, 1, 2]

            @pl.when(y != p)
            def _():
                y_copy(p, y).start()

        @pl.when(jnp.logical_and(phase == 3, jnp.logical_and(quarter >= 11, quarter <= 23)))
        def _():
            p = round_of - 2
            for level, step in both:
                first_copy(p, level, step).wait_recv()
            middle[p, 0] = chip_sum[p, 0, :, x] + first_in[p, 0, 0] + first_in[p, 0, 1] + first_in[p, 0, 2]
            middle[p, 1] = chip_sum[p, 1, z] + first_in[p, 1, 0] + first_in[p, 1, 1] + first_in[p, 1, 2]
            for level, step in both:
                second_copy(p, level, step).start()

        @pl.when(jnp.logical_and(phase == 3, y == round_of - 4))
        def _():
            solve_forward()

    def spread(p, level, step):
        chunk = x_ref.at[p, level, z, x, core]
        device = on_y(lax.rem(y + step, PAIRS))
        return remote(chunk, chunk, spread_s.at[level, step - 1], spread_r.at[p, level], device)

    def send_level(level, value):
        x_ref[y, level, z, x, core] = value
        for step in (3, 1, 2):
            spread(y, level, step).start()

    def solve_backward(first, second):
        second = small_products([split(second) + top_parts(1, 2 * y + 1)], False)
        send_level(1, second)
        first = first - small_products([split(second) + top_parts(0, 2 * y + 1)], False)
        send_level(0, small_products([split(first) + top_parts(0, 2 * y)], False))

    def chunk_copy(p, level, step):
        chunk = x_ref.at[p, level, z, x, core]
        device = on_z(step) if level == 0 else on_x(step)
        return remote(chunk, chunk, chunk_s.at[p, level, step - 1], chunk_r.at[p, level, step - 1], device)

    def line_copy(p, level, step):
        if level == 0:
            line, device = x_ref.at[p, 0, :, x, core], on_x(step)
        else:
            line, device = x_ref.at[p, 1, z, :, core], on_z(step)
        return remote(line, line, line_s.at[p, level, step - 1], line_r.at[p, level, step - 1], device)

    def send_lines(p):
        for level, step in both:
            chunk_copy(p, level, step).wait_recv()
        for level, step in both:
            line_copy(p, level, step).start()

    def swap_copy(p, half):
        part = x_ref.at[p, :, :, :, half]
        return remote(part, part, swap_s.at[p], swap_r.at[p], mate)

    def send_swap(p):
        for level, step in both:
            line_copy(p, level, step).wait_recv()
        swap_copy(p, core).start()

    def subtract(p, level):
        parts = split(x_ref[p, level, z, x, core])
        return [
            solved[column] - small_products([parts + top_parts(column, 2 * p + level)], False) for column in range(2)
        ]

    def arrive(p):
        def take_level(level):
            @pl.when(y != p)
            def _():
                spread(p, level, 1).wait_recv()

        take_level(1)
        for step in (2, 1, 3):
            chunk_copy(p, 1, step).start()
        if p > 0:

            @pl.when(y < p)
            def _():
                solved[0], solved[1] = subtract(p, 1)

        take_level(0)
        if p > 0:

            @pl.when(y == p - 1)
            def _():
                solve_backward(*subtract(p, 0))

        if p > 1:

            @pl.when(y < p - 1)
            def _():
                solved[0], solved[1] = subtract(p, 0)

        for step in (2, 1, 3):
            chunk_copy(p, 0, step).start()

    def take(p, half):
        for level in range(2):
            high, low = split(x_ref[p, level, :, :, half].reshape(256, 256))
            x_high[level] = high
            x_low[level] = low

    def out_copy(k):
        return pltpu.make_async_copy(z_ref.at[k], z_out.at[k], out_sem.at[k])

    def correct(p, half, leave=False):
        @pl.loop(0, LEAVES // GROUP)
        def _(group):
            for k in [GROUP * group + i for i in range(GROUP)]:
                pieces = []
                for level in range(2):
                    place = place_of(k, 2 * p + level)
                    pieces.append((x_high[level], x_low[level], slot_high[place], slot_low[place]))
                part = z_ref[k, :, half].reshape(256, 256) - products(pieces, False)
                z_ref[k, :, half] = part.reshape(16, HALF, 256)
                if leave:
                    out_copy(k).start()

    def own_half(p):
        take(p, core)
        correct(p, core)

    def other_half(p):
        swap_copy(p, other).wait_recv()
        if p == 0:
            own_copy.start()
        take(p, other)
        correct(p, other, leave=p == 0)

    @pl.when(y == PAIRS - 1)
    def _():
        solve_backward(solved[0], solved[1])

    arrive(3)
    arrive(2)
    send_lines(3)
    arrive(1)
    send_lines(2)
    send_swap(3)
    arrive(0)
    send_lines(1)
    own_half(3)
    send_swap(2)
    other_half(3)
    send_lines(0)
    own_half(2)
    send_swap(1)
    other_half(2)
    own_half(1)
    other_half(1)
    send_swap(0)
    own_half(0)
    other_half(0)

    own_copy.wait()
    for k in range(LEAVES):
        out_copy(k).wait()
    rhs_copy.wait_send()
    blocks_copy.wait_send()
    for p in range(PAIRS):
        pair_copy(p).wait_send()
        for level, step in both:
            first_copy(p, level, step).wait_send()
            second_copy(p, level, step).wait_send()
            chunk_copy(p, level, step).wait_send()
            line_copy(p, level, step).wait_send()
        swap_copy(p, core).wait_send()

        @pl.when(y != p)
        def _():
            y_copy(p, y).wait_send()

    for chip in range(1, PAIRS):

        @pl.when(y < chip)
        def _():
            update_copy(y, chip).wait_send()

    for step in range(1, PAIRS):
        for level in range(2):
            spread(y, level, step).wait_send()


def whole_solve(targets, live, leaf_rhs, leaf_inverse, leaf_blocks, rhs, top_blocks):
    dma = pltpu.SemaphoreType.DMA
    hbm = pl.BlockSpec(memory_space=pl.ANY)
    return pl.pallas_call(
        whole_kernel,
        out_shape=(
            jax.ShapeDtypeStruct((LEAVES, 16, 2, HALF, 256), f32),
            jax.ShapeDtypeStruct((2, HALF, 256), f32),
        ),
        in_specs=[hbm] * 7,
        out_specs=(hbm, hbm),
        scratch_shapes=[
            pltpu.SMEM((SLOTS, LEAVES), jnp.int32),
            pltpu.SMEM((LEAVES,), jnp.int32),
            pltpu.VMEM((LEAVES, 16, 2, HALF, 256), f32),
            pltpu.VMEM((LEAVES, 256, 256), f32),
            pltpu.VMEM((LEAVES * SLOTS, 256, 256), f32),
            pltpu.VMEM((LEAVES * SLOTS + 1, 256, 256), bf16),
            pltpu.VMEM((LEAVES * SLOTS + 1, 256, 256), bf16),
            pltpu.VMEM((LEAVES, 512, 256), bf16),
            pltpu.VMEM((LEAVES, 512, 256), bf16),
            pltpu.VMEM((PAIRS, 2, 4, 4, 2, HALF, 256), f32),
            pltpu.VMEM((PAIRS, 2, 4, 4, 2, HALF, 256), f32),
            pltpu.VMEM((2, 256, 256), bf16),
            pltpu.VMEM((2, 256, 256), bf16),
            pltpu.VMEM((2, 8, 256, 256), f32),
            pltpu.VMEM((2, 8, 256, 256), bf16),
            pltpu.VMEM((2, 8, 256, 256), bf16),
            pltpu.VMEM((PAIRS, 2, 4, 4, HALF, 256), f32),
            pltpu.VMEM((PAIRS, 2, 4, 4, HALF, 256), f32),
            pltpu.VMEM((PAIRS, 2, 3, 4, HALF, 256), f32),
            pltpu.VMEM((PAIRS, 2, 4, HALF, 256), f32),
            pltpu.VMEM((PAIRS, 2, 3, HALF, 256), f32),
            pltpu.VMEM((PAIRS, 2, HALF, 256), f32),
            pltpu.VMEM((PAIRS, 2, HALF, 256), f32),
            pltpu.VMEM((PAIRS, 2, HALF, 256), f32),
            pltpu.VMEM((PAIRS, 2, HALF, 256), f32),
            pltpu.VMEM((2, HALF, 256), f32),
            pltpu.VMEM((2, HALF, 256), f32),
            dma((LEAVES,)), dma((LEAVES,)), dma((LEAVES,)), dma((LEAVES,)),
            dma((2,)), dma((2,)), dma,
            dma, dma, dma, dma,
            dma((PAIRS,)), dma((PAIRS,)),
            dma((PAIRS, 2, 3)), dma((PAIRS, 2, 3)),
            dma((PAIRS, 2, 3)), dma((PAIRS, 2, 3)),
            dma((PAIRS,)), dma((PAIRS,)),
            dma((PAIRS,)), dma((PAIRS,)),
            dma((2, 3)), dma((PAIRS, 2)),
            dma((PAIRS, 2, 3)), dma((PAIRS, 2, 3)),
            dma((PAIRS, 2, 3)), dma((PAIRS, 2, 3)),
            dma((PAIRS,)), dma((PAIRS,)),
        ],
        compiler_params=pltpu.CompilerParams(
            collective_id=0, has_side_effects=True, vmem_limit_bytes=60 * 1024 * 1024
        ),
        cost_estimate=pl.CostEstimate(flops=3 * 10**10, bytes_accessed=2 * 10**7, transcendentals=0),
    )(targets, live, leaf_rhs, leaf_inverse, leaf_blocks, rhs, top_blocks)


def last_kernel(z_hbm, inverse_hbm, out_hbm, z_ref, inverse_ref, out_ref, z_sem, inverse_sem, out_sem):
    def copies(k):
        return (
            pltpu.make_async_copy(z_hbm.at[k], z_ref.at[k], z_sem.at[k]),
            pltpu.make_async_copy(inverse_hbm.at[k], inverse_ref.at[k], inverse_sem.at[k]),
        )

    def out_copy(k):
        column = pl.ds(pl.multiple_of(k * 256, 256), 256)
        return pltpu.make_async_copy(out_ref.at[k], out_hbm.at[:, column], out_sem.at[k])

    for k in range(LEAVES):
        for copy in copies(k):
            copy.start()

    @pl.loop(0, LEAVES)
    def _(k):
        for copy in copies(k):
            copy.wait()
        parts = split(inverse_ref[k])
        for part in range(2):
            rows = pl.ds(256 * part, 256)
            out_ref[k, rows] = products([split(z_ref[k, rows]) + parts], False)
        out_copy(k).start()

    for k in range(LEAVES):
        out_copy(k).wait()


def last_product(z, inverse):
    hbm = pl.BlockSpec(memory_space=pl.ANY)
    dma = pltpu.SemaphoreType.DMA
    return pl.pallas_call(
        last_kernel,
        out_shape=jax.ShapeDtypeStruct((512, LEAVES * 256), f32),
        in_specs=[hbm, hbm],
        out_specs=hbm,
        scratch_shapes=[
            pltpu.VMEM((LEAVES, 512, 256), f32),
            pltpu.VMEM((LEAVES, 256, 256), f32),
            pltpu.VMEM((LEAVES, 512, 256), f32),
            dma((LEAVES,)), dma((LEAVES,)), dma((LEAVES,)),
        ],
        compiler_params=pltpu.CompilerParams(vmem_limit_bytes=60 * 1024 * 1024),
        cost_estimate=pl.CostEstimate(flops=16 * 10**8, bytes_accessed=10**7, transcendentals=0),
    )(z, inverse)


def on_device(leaf_rhs, top_rhs, leaf_inverse, leaf_blocks, leaf_targets, leaf_live, top_blocks):
    z, own = whole_solve(
        leaf_targets.T, leaf_live, leaf_rhs.reshape(16, 2, HALF, LEAVES * 256), leaf_inverse, leaf_blocks.reshape(LEAVES * SLOTS, 256, 256),
        top_rhs.reshape(2, HALF, 256), top_blocks[0],
    )
    return (last_product(z.reshape(LEAVES, 512, 256), leaf_inverse), own.reshape(2 * HALF, 256))


def solution(mesh):
    in_specs = (
        P(None, ("row", "col")),
        P("col", "row"),
        P(("row", "col"), None, None),
        P(("row", "col"), None, None, None),
        P(("row", "col"), None),
        P(("row", "col")),
        P("row", None, None, None),
    )
    out_specs = (P(None, ("row", "col")), P("col", "row"))
    return jax.shard_map(
        on_device, mesh=mesh, in_specs=in_specs, out_specs=out_specs, check_vma=False
    )
```

```python
import jax
import jax.numpy as jnp
from jax import lax
from jax.experimental import pallas as pl
from jax.experimental.pallas import tpu as pltpu
from jax.sharding import PartitionSpec as P

MESH = pl.DeviceIdType.MESH
f32 = jnp.float32
bf16 = jnp.bfloat16

PAIRS = 4
HALF = 16
LEAVES = 8
SLOTS = 4
GROUP = 8
EMPTY = LEAVES * SLOTS


def split(value):
    high = value.astype(bf16)
    return high, (value - high.astype(f32)).astype(bf16)


def products(pieces, transposed):
    left, right = [], []
    for a_high, a_low, b_high, b_low in pieces:
        left += [a_high, a_high, a_low]
        right += [b_high, b_low, b_high]
    axis = 1 if transposed else 0
    return lax.dot_general(
        jnp.concatenate(left, axis=1), jnp.concatenate(right, axis=axis),
        (((1,), (axis,)), ((), ())), preferred_element_type=f32,
    )


def small_products(pieces, transposed):
    axis = 1 if transposed else 0
    dims = (((1,), (axis,)), ((), ()))
    high = jnp.concatenate([piece[0] for piece in pieces], axis=1)
    both = jnp.concatenate([high, jnp.concatenate([piece[1] for piece in pieces], axis=1)], axis=0)
    b_high = jnp.concatenate([piece[2] for piece in pieces], axis=axis)
    b_low = jnp.concatenate([piece[3] for piece in pieces], axis=axis)
    upper = lax.dot_general(both, b_high, dims, preferred_element_type=f32)
    lower = lax.dot_general(high, b_low, dims, preferred_element_type=f32)
    return upper[:HALF] + upper[HALF:] + lower


def whole_kernel(
    targets_ref, live_ref, leaf_rhs, leaf_inverse, leaf_blocks, rhs_ref, top_ref, z_out, own_out,
    targets, live, z_ref, inverse, slots, slot_high, slot_low, y_high, y_low, u_ref, x_ref, x_high, x_low, top, top_high, top_low,
    pair_in, chip_sum, first_in, middle, second_in, plane_sum, y_in, update_out, update_in, rhs, solved,
    leaf_sem, inverse_sem, slots_sem, out_sem, local_sem, index_sem, own_sem, blocks_s, blocks_r, rhs_s, rhs_r, pair_s, pair_r,
    first_s, first_r, second_s, second_r, y_s, y_r, update_s, update_r,
    spread_s, spread_r, chunk_s, chunk_r, line_s, line_r, swap_s, swap_r,
):
    row = lax.axis_index("row")
    col = lax.axis_index("col")
    core = lax.rem(row, 2)
    y = lax.div(row, 2)
    other = 1 - core
    z = lax.div(col, 4)
    x = lax.rem(col, 4)
    mate = {"row": 2 * y + other}

    def on_y(chip):
        return {"row": 2 * chip + core}

    def on_x(step):
        return {"col": 4 * z + lax.rem(x + step, 4)}

    def on_z(step):
        return {"col": 4 * lax.rem(z + step, 4) + x}

    def remote(src, dst, send, recv, device):
        return pltpu.make_async_remote_copy(
            src_ref=src, dst_ref=dst, send_sem=send, recv_sem=recv, device_id=device, device_id_type=MESH
        )

    barrier = pltpu.get_barrier_semaphore()
    pl.semaphore_signal(barrier, inc=1, device_id=mate, device_id_type=MESH)
    for step in range(1, PAIRS):
        pl.semaphore_signal(barrier, inc=1, device_id=on_y(lax.rem(y + step, PAIRS)), device_id_type=MESH)
    for step in range(1, 4):
        pl.semaphore_signal(barrier, inc=1, device_id=on_x(step), device_id_type=MESH)
        pl.semaphore_signal(barrier, inc=1, device_id=on_z(step), device_id_type=MESH)

    def leaf_copies(k):
        column = pl.ds(pl.multiple_of(k * 256, 256), 256)
        group = pl.ds(SLOTS * k, SLOTS)
        return (
            pltpu.make_async_copy(leaf_rhs.at[:, :, :, column], z_ref.at[k], leaf_sem.at[k]),
            pltpu.make_async_copy(leaf_inverse.at[k], inverse.at[k], inverse_sem.at[k]),
            pltpu.make_async_copy(leaf_blocks.at[group], slots.at[group], slots_sem.at[k]),
        )

    index_copies = (
        pltpu.make_async_copy(targets_ref, targets, index_sem.at[0]),
        pltpu.make_async_copy(live_ref, live, index_sem.at[1]),
    )
    for copy in index_copies:
        copy.start()
    for k in range(LEAVES):
        for copy in leaf_copies(k):
            copy.start()
    local_copies = (
        pltpu.make_async_copy(top_ref, top.at[core], local_sem.at[0]),
        pltpu.make_async_copy(rhs_ref.at[core], rhs.at[core], local_sem.at[1]),
    )
    for copy in local_copies:
        copy.start()
    own_copy = pltpu.make_async_copy(x_ref.at[y, core, z, x], own_out, own_sem)
    zero_block = jnp.zeros((256, 256), bf16)
    slot_high[EMPTY] = zero_block
    slot_low[EMPTY] = zero_block

    @pl.loop(0, LEAVES)
    def _(k):
        for copy in leaf_copies(k):
            copy.wait()
        b_high, b_low = split(inverse[k])
        for part in range(2):
            rows = pl.ds(256 * part, 256)
            groups = pl.ds(8 * part, 8)
            a_high, a_low = split(z_ref[k, groups].reshape(256, 256))
            result = products([(a_high, a_low, b_high, b_low)], True)
            z_ref[k, groups] = result.reshape(8, 2, HALF, 256)
            high, low = split(result)
            y_high[k, rows] = high
            y_low[k, rows] = low
        for j in range(SLOTS):
            high, low = split(slots[SLOTS * k + j])
            slot_high[SLOTS * k + j] = high
            slot_low[SLOTS * k + j] = low

    for copy in index_copies:
        copy.wait()
    pl.semaphore_wait(barrier, 10)
    blocks_copy = remote(top_ref, top.at[core], blocks_s, blocks_r, mate)
    blocks_copy.start()
    rhs_copy = remote(rhs_ref.at[other], rhs.at[core], rhs_s, rhs_r, mate)
    rhs_copy.start()

    def place_of(k, level):
        place = jnp.int32(EMPTY)
        for j in range(SLOTS):
            used = jnp.logical_and(targets[j, k] == level, live[k] > j)
            place = jnp.where(used, SLOTS * k + j, place)
        return place

    def pair_copy(p):
        return remote(u_ref.at[p, :, :, :, other], pair_in.at[p], pair_s.at[p], pair_r.at[p], mate)

    def first_copy(p, level, step):
        if level == 0:
            src, device = chip_sum.at[p, 0, :, lax.rem(x + step, 4)], on_x(step)
        else:
            src, device = chip_sum.at[p, 1, lax.rem(z + step, 4)], on_z(step)
        return remote(
            src, first_in.at[p, level, step - 1], first_s.at[p, level, step - 1], first_r.at[p, level, step - 1], device
        )

    def second_copy(p, level, step):
        if level == 0:
            src, device = middle.at[p, 0, lax.rem(z + step, 4)], on_z(step)
        else:
            src, device = middle.at[p, 1, lax.rem(x + step, 4)], on_x(step)
        return remote(
            src, second_in.at[p, level, step - 1],
            second_s.at[p, level, step - 1], second_r.at[p, level, step - 1], device,
        )

    def y_copy(p, source):
        return remote(plane_sum.at[p], y_in.at[source], y_s.at[p], y_r.at[source], on_y(p))

    both = [(level, step) for step in (2, 1, 3) for level in range(2)]

    def update_copy(source, target):
        return remote(update_out.at[target], update_in.at[source], update_s.at[target], update_r.at[source], on_y(target))

    def top_parts(column, level):
        return top_high[column, level], top_low[column, level]

    def solve_forward():
        y_in[y] = jnp.zeros((2, HALF, 256), f32)
        for chip in range(PAIRS):

            @pl.when(y != chip)
            def _():
                y_copy(chip, chip).wait_recv()

        solved[...] = rhs[...] - plane_sum[y] - (y_in[0] + y_in[1] + y_in[2] + y_in[3])
        for chip in range(PAIRS - 1):

            @pl.when(y > chip)
            def _():
                update_copy(chip, y).wait_recv()
                solved[...] = solved[...] - update_in[chip]

        first = small_products([split(solved[0]) + top_parts(0, 2 * y)], True)
        first_parts = split(first)
        second = solved[1] - small_products([first_parts + top_parts(0, 2 * y + 1)], True)
        second = small_products([split(second) + top_parts(1, 2 * y + 1)], True)
        second_parts = split(second)
        solved[0] = first
        solved[1] = second

        def update(chip):
            for level in range(2):
                update_out[chip, level] = small_products(
                    [
                        first_parts + top_parts(0, 2 * chip + level),
                        second_parts + top_parts(1, 2 * chip + level),
                    ],
                    True,
                )

        update(lax.rem(y + 1, PAIRS))

        @pl.when(y < PAIRS - 1)
        def _():
            update_copy(y, lax.rem(y + 1, PAIRS)).start()

        for chip in range(2, PAIRS):

            @pl.when(y < chip - 1)
            def _():
                update(chip)
                update_copy(y, chip).start()

    @pl.loop(0, 32)
    def _(quarter):
        phase = lax.rem(quarter, 4)
        round_of = lax.div(quarter, 4)

        @pl.when(quarter < 16)
        def _():
            level = lax.rem(lax.div(quarter, 2), 2)
            part = lax.rem(quarter, 2)
            rows = pl.ds(pl.multiple_of(256 * part, 256), 256)
            pieces = []
            for k in range(LEAVES):
                place = place_of(k, 2 * round_of + level)
                pieces.append((y_high[k, rows], y_low[k, rows], slot_high[place], slot_low[place]))
            u_ref[round_of, level, pl.ds(2 * part, 2)] = products(pieces, True).reshape(2, 4, 2, HALF, 256)

            @pl.when(phase == 3)
            def _():
                pair_copy(round_of).start()

        @pl.when(jnp.logical_and(phase == 0, jnp.logical_and(quarter >= 4, quarter <= 16)))
        def _():
            p = round_of - 1
            pair_copy(p).wait_recv()
            chip_sum[p] = u_ref[p, :, :, :, core] + pair_in[p]
            for level, step in both:
                first_copy(p, level, step).start()

        @pl.when(quarter == 18)
        def _():
            rhs_copy.wait_recv()
            remote(top_ref, top.at[other], blocks_s, blocks_r, mate).wait_recv()
            for copy in local_copies:
                copy.wait()
            for column in range(2):

                @pl.loop(0, 8)
                def _(level):
                    high, low = split(top[column, level])
                    top_high[column, level] = high
                    top_low[column, level] = low

        @pl.when(jnp.logical_and(phase == 3, jnp.logical_and(quarter >= 15, quarter <= 27)))
        def _():
            p = round_of - 3
            for level, step in both:
                second_copy(p, level, step).wait_recv()
            plane_sum[p, 0] = middle[p, 0, z] + second_in[p, 0, 0] + second_in[p, 0, 1] + second_in[p, 0, 2]
            plane_sum[p, 1] = middle[p, 1, x] + second_in[p, 1, 0] + second_in[p, 1, 1] + second_in[p, 1, 2]

            @pl.when(y != p)
            def _():
                y_copy(p, y).start()

        @pl.when(jnp.logical_and(phase == 3, jnp.logical_and(quarter >= 11, quarter <= 23)))
        def _():
            p = round_of - 2
            for level, step in both:
                first_copy(p, level, step).wait_recv()
            middle[p, 0] = chip_sum[p, 0, :, x] + first_in[p, 0, 0] + first_in[p, 0, 1] + first_in[p, 0, 2]
            middle[p, 1] = chip_sum[p, 1, z] + first_in[p, 1, 0] + first_in[p, 1, 1] + first_in[p, 1, 2]
            for level, step in both:
                second_copy(p, level, step).start()

        @pl.when(jnp.logical_and(phase == 3, y == round_of - 4))
        def _():
            solve_forward()

    def spread(p, level, step):
        chunk = x_ref.at[p, level, z, x, core]
        device = on_y(lax.rem(y + step, PAIRS))
        return remote(chunk, chunk, spread_s.at[level, step - 1], spread_r.at[p, level], device)

    def send_level(level, value):
        x_ref[y, level, z, x, core] = value
        for step in (3, 1, 2):
            spread(y, level, step).start()

    def solve_backward(first, second):
        second = small_products([split(second) + top_parts(1, 2 * y + 1)], False)
        send_level(1, second)
        first = first - small_products([split(second) + top_parts(0, 2 * y + 1)], False)
        send_level(0, small_products([split(first) + top_parts(0, 2 * y)], False))

    def chunk_copy(p, level, step):
        chunk = x_ref.at[p, level, z, x, core]
        device = on_z(step) if level == 0 else on_x(step)
        return remote(chunk, chunk, chunk_s.at[p, level, step - 1], chunk_r.at[p, level, step - 1], device)

    def line_copy(p, level, step):
        if level == 0:
            line, device = x_ref.at[p, 0, :, x, core], on_x(step)
        else:
            line, device = x_ref.at[p, 1, z, :, core], on_z(step)
        return remote(line, line, line_s.at[p, level, step - 1], line_r.at[p, level, step - 1], device)

    def send_lines(p):
        for level, step in both:
            chunk_copy(p, level, step).wait_recv()
        for level, step in both:
            line_copy(p, level, step).start()

    def swap_copy(p, half):
        part = x_ref.at[p, :, :, :, half]
        return remote(part, part, swap_s.at[p], swap_r.at[p], mate)

    def send_swap(p):
        for level, step in both:
            line_copy(p, level, step).wait_recv()
        swap_copy(p, core).start()

    def subtract(p, level):
        parts = split(x_ref[p, level, z, x, core])
        return [
            solved[column] - small_products([parts + top_parts(column, 2 * p + level)], False) for column in range(2)
        ]

    def arrive(p):
        def take_level(level):
            @pl.when(y != p)
            def _():
                spread(p, level, 1).wait_recv()

        take_level(1)
        if p > 0:

            @pl.when(y < p)
            def _():
                solved[0], solved[1] = subtract(p, 1)

        take_level(0)
        if p > 0:

            @pl.when(y == p - 1)
            def _():
                solve_backward(*subtract(p, 0))

        if p > 1:

            @pl.when(y < p - 1)
            def _():
                solved[0], solved[1] = subtract(p, 0)

        for step in (2, 1, 3):
            chunk_copy(p, 1, step).start()
        for step in (2, 1, 3):
            chunk_copy(p, 0, step).start()

    def take(p, half):
        for level in range(2):
            high, low = split(x_ref[p, level, :, :, half].reshape(256, 256))
            x_high[level] = high
            x_low[level] = low

    def out_copy(k):
        return pltpu.make_async_copy(z_ref.at[k], z_out.at[k], out_sem.at[k])

    def correct(p, half, leave=False):
        @pl.loop(0, LEAVES // GROUP)
        def _(group):
            for k in [GROUP * group + i for i in range(GROUP)]:
                pieces = []
                for level in range(2):
                    place = place_of(k, 2 * p + level)
                    pieces.append((x_high[level], x_low[level], slot_high[place], slot_low[place]))
                part = z_ref[k, :, half].reshape(256, 256) - products(pieces, False)
                z_ref[k, :, half] = part.reshape(16, HALF, 256)
                if leave:
                    out_copy(k).start()

    def own_half(p):
        take(p, core)
        correct(p, core)

    def other_half(p):
        swap_copy(p, other).wait_recv()
        if p == 0:
            own_copy.start()
        take(p, other)
        correct(p, other, leave=p == 0)

    @pl.when(y == PAIRS - 1)
    def _():
        solve_backward(solved[0], solved[1])

    arrive(3)
    arrive(2)
    send_lines(3)
    arrive(1)
    send_lines(2)
    send_swap(3)
    arrive(0)
    send_lines(1)
    own_half(3)
    send_swap(2)
    other_half(3)
    send_lines(0)
    own_half(2)
    send_swap(1)
    other_half(2)
    own_half(1)
    other_half(1)
    send_swap(0)
    own_half(0)
    other_half(0)

    own_copy.wait()
    for k in range(LEAVES):
        out_copy(k).wait()
    rhs_copy.wait_send()
    blocks_copy.wait_send()
    for p in range(PAIRS):
        pair_copy(p).wait_send()
        for level, step in both:
            first_copy(p, level, step).wait_send()
            second_copy(p, level, step).wait_send()
            chunk_copy(p, level, step).wait_send()
            line_copy(p, level, step).wait_send()
        swap_copy(p, core).wait_send()

        @pl.when(y != p)
        def _():
            y_copy(p, y).wait_send()

    for chip in range(1, PAIRS):

        @pl.when(y < chip)
        def _():
            update_copy(y, chip).wait_send()

    for step in range(1, PAIRS):
        for level in range(2):
            spread(y, level, step).wait_send()


def whole_solve(targets, live, leaf_rhs, leaf_inverse, leaf_blocks, rhs, top_blocks):
    dma = pltpu.SemaphoreType.DMA
    hbm = pl.BlockSpec(memory_space=pl.ANY)
    return pl.pallas_call(
        whole_kernel,
        out_shape=(
            jax.ShapeDtypeStruct((LEAVES, 16, 2, HALF, 256), f32),
            jax.ShapeDtypeStruct((2, HALF, 256), f32),
        ),
        in_specs=[hbm] * 7,
        out_specs=(hbm, hbm),
        scratch_shapes=[
            pltpu.SMEM((SLOTS, LEAVES), jnp.int32),
            pltpu.SMEM((LEAVES,), jnp.int32),
            pltpu.VMEM((LEAVES, 16, 2, HALF, 256), f32),
            pltpu.VMEM((LEAVES, 256, 256), f32),
            pltpu.VMEM((LEAVES * SLOTS, 256, 256), f32),
            pltpu.VMEM((LEAVES * SLOTS + 1, 256, 256), bf16),
            pltpu.VMEM((LEAVES * SLOTS + 1, 256, 256), bf16),
            pltpu.VMEM((LEAVES, 512, 256), bf16),
            pltpu.VMEM((LEAVES, 512, 256), bf16),
            pltpu.VMEM((PAIRS, 2, 4, 4, 2, HALF, 256), f32),
            pltpu.VMEM((PAIRS, 2, 4, 4, 2, HALF, 256), f32),
            pltpu.VMEM((2, 256, 256), bf16),
            pltpu.VMEM((2, 256, 256), bf16),
            pltpu.VMEM((2, 8, 256, 256), f32),
            pltpu.VMEM((2, 8, 256, 256), bf16),
            pltpu.VMEM((2, 8, 256, 256), bf16),
            pltpu.VMEM((PAIRS, 2, 4, 4, HALF, 256), f32),
            pltpu.VMEM((PAIRS, 2, 4, 4, HALF, 256), f32),
            pltpu.VMEM((PAIRS, 2, 3, 4, HALF, 256), f32),
            pltpu.VMEM((PAIRS, 2, 4, HALF, 256), f32),
            pltpu.VMEM((PAIRS, 2, 3, HALF, 256), f32),
            pltpu.VMEM((PAIRS, 2, HALF, 256), f32),
            pltpu.VMEM((PAIRS, 2, HALF, 256), f32),
            pltpu.VMEM((PAIRS, 2, HALF, 256), f32),
            pltpu.VMEM((PAIRS, 2, HALF, 256), f32),
            pltpu.VMEM((2, HALF, 256), f32),
            pltpu.VMEM((2, HALF, 256), f32),
            dma((LEAVES,)), dma((LEAVES,)), dma((LEAVES,)), dma((LEAVES,)),
            dma((2,)), dma((2,)), dma,
            dma, dma, dma, dma,
            dma((PAIRS,)), dma((PAIRS,)),
            dma((PAIRS, 2, 3)), dma((PAIRS, 2, 3)),
            dma((PAIRS, 2, 3)), dma((PAIRS, 2, 3)),
            dma((PAIRS,)), dma((PAIRS,)),
            dma((PAIRS,)), dma((PAIRS,)),
            dma((2, 3)), dma((PAIRS, 2)),
            dma((PAIRS, 2, 3)), dma((PAIRS, 2, 3)),
            dma((PAIRS, 2, 3)), dma((PAIRS, 2, 3)),
            dma((PAIRS,)), dma((PAIRS,)),
        ],
        compiler_params=pltpu.CompilerParams(
            collective_id=0, has_side_effects=True, vmem_limit_bytes=60 * 1024 * 1024
        ),
        cost_estimate=pl.CostEstimate(flops=3 * 10**10, bytes_accessed=2 * 10**7, transcendentals=0),
    )(targets, live, leaf_rhs, leaf_inverse, leaf_blocks, rhs, top_blocks)


def last_kernel(z_hbm, inverse_hbm, out_hbm, z_ref, inverse_ref, out_ref, z_sem, inverse_sem, out_sem):
    def copies(k):
        return (
            pltpu.make_async_copy(z_hbm.at[k], z_ref.at[k], z_sem.at[k]),
            pltpu.make_async_copy(inverse_hbm.at[k], inverse_ref.at[k], inverse_sem.at[k]),
        )

    def out_copy(k):
        column = pl.ds(pl.multiple_of(k * 256, 256), 256)
        return pltpu.make_async_copy(out_ref.at[k], out_hbm.at[:, column], out_sem.at[k])

    for k in range(LEAVES):
        for copy in copies(k):
            copy.start()

    @pl.loop(0, LEAVES)
    def _(k):
        for copy in copies(k):
            copy.wait()
        parts = split(inverse_ref[k])
        for part in range(2):
            rows = pl.ds(256 * part, 256)
            out_ref[k, rows] = products([split(z_ref[k, rows]) + parts], False)
        out_copy(k).start()

    for k in range(LEAVES):
        out_copy(k).wait()


def last_product(z, inverse):
    hbm = pl.BlockSpec(memory_space=pl.ANY)
    dma = pltpu.SemaphoreType.DMA
    return pl.pallas_call(
        last_kernel,
        out_shape=jax.ShapeDtypeStruct((512, LEAVES * 256), f32),
        in_specs=[hbm, hbm],
        out_specs=hbm,
        scratch_shapes=[
            pltpu.VMEM((LEAVES, 512, 256), f32),
            pltpu.VMEM((LEAVES, 256, 256), f32),
            pltpu.VMEM((LEAVES, 512, 256), f32),
            dma((LEAVES,)), dma((LEAVES,)), dma((LEAVES,)),
        ],
        compiler_params=pltpu.CompilerParams(vmem_limit_bytes=60 * 1024 * 1024),
        cost_estimate=pl.CostEstimate(flops=16 * 10**8, bytes_accessed=10**7, transcendentals=0),
    )(z, inverse)


def on_device(leaf_rhs, top_rhs, leaf_inverse, leaf_blocks, leaf_targets, leaf_live, top_blocks):
    z, own = whole_solve(
        leaf_targets.T, leaf_live, leaf_rhs.reshape(16, 2, HALF, LEAVES * 256), leaf_inverse, leaf_blocks.reshape(LEAVES * SLOTS, 256, 256),
        top_rhs.reshape(2, HALF, 256), top_blocks[0],
    )
    return (last_product(z.reshape(LEAVES, 512, 256), leaf_inverse), own.reshape(2 * HALF, 256))


def solution(mesh):
    in_specs = (
        P(None, ("row", "col")),
        P("col", "row"),
        P(("row", "col"), None, None),
        P(("row", "col"), None, None, None),
        P(("row", "col"), None),
        P(("row", "col")),
        P("row", None, None, None),
    )
    out_specs = (P(None, ("row", "col")), P("col", "row"))
    return jax.shard_map(
        on_device, mesh=mesh, in_specs=in_specs, out_specs=out_specs, check_vma=False
    )
```
